256 devices in a mesh: lon: 32 (over z, y), lat: 4 (over x), dep: 2 (over core).
Axes of the slice: x: 4, y: 4, z: 8, core: 2. Of those that a mesh axis runs over, the one named last changes fastest.
Arguments:
- adjoint_u: float32 [64, 128, 4096], P('dep', 'lat', 'lon'), may hold values from -6 to 6
- adjoint_v: float32 [64, 128, 4096], P('dep', 'lat', 'lon'), may hold values from -6 to 6
- adjoint_t: float32 [64, 128, 4096], P('dep', 'lat', 'lon'), may hold values from -6 to 6
- zonal_vel: float32 [64, 128, 4096], P('dep', 'lat', 'lon'), may hold values from -1.5 to 1.5
- merid_vel: float32 [64, 128, 4096], P('dep', 'lat', 'lon'), may hold values from -1.5 to 1.5
- coriolis_dt: float32 [128], P('lat'), may hold values from -0.8 to 0.8
- layer_thick: float32 [64], P('dep'), may hold values from 0.5 to 2
- overturn_weight: float32 [64, 128], P(None, 'lat'), may hold values from 0.3 to 3
- overturn_target: float32 [64, 128], P(None, 'lat'), may hold values from -5 to 5
- atlantic: int32 [128, 4096], P('lat', 'lon'), may hold values from 0 to 1, as said below
- bottom_level: int32 [128, 4096], P('lat', 'lon'), may hold values from 0 to 64
Outputs:
- result_u: float32 [64, 128, 4096], P('dep', 'lat', 'lon')
- result_v: float32 [64, 128, 4096], P('dep', 'lat', 'lon')
- result_t: float32 [64, 128, 4096], P('dep', 'lat', 'lon')
The draws below stay inside these ranges and needn't reach their ends.
Inputs may be any that keep to these rules, and one draw needn't show every extreme that they name: `atlantic`: in each latitude row the basin is one run of consecutive longitudes, possibly continuing across the seam at longitude 0. `bottom_level`: 0 marks land.
All inputs are finite; a program needn't handle non-finite values.
Results may differ from the reference program's by a relative error of at most 0.00002.
Values sent between devices are 32-bit elements; how exact they have to be, the bound alone decides.
A program may use at most 64 MiB of HBM per device.

```python
import math
import jax
import jax.numpy as jnp
from jax import lax

ITERS = 8
NX = 4096
NY = 128
NZ = 64


def draw_atlantic(key, part):
    key = jax.random.fold_in(key, 7)
    first_key, second_key = jax.random.split(key)
    western = jax.random.randint(first_key, (NY,), 0, NX)
    extent = jax.random.randint(second_key, (NY,), NX // 4, NX // 2)
    columns = jnp.arange(NX, dtype=jnp.int32)
    offset = (columns[None, :] - western[:, None]) % NX
    return (offset < extent[:, None]).astype(jnp.int32)


def plant(drawn, own_key, least, high):
    spot = [jax.random.randint(jax.random.fold_in(own_key, axis), (), 0, length) for axis, length in enumerate(drawn.shape)]
    main_axis = drawn.shape.index(max(drawn.shape))
    neighbour = spot[:main_axis] + [(spot[main_axis] + 1) % drawn.shape[main_axis]] + spot[main_axis + 1:]
    return drawn.at[tuple(spot)].set(least).at[tuple(neighbour)].set(high)


def block_levels(stream_key, shape, cuts, smallest, largest):
    def one(axis_at, blocks):
        heights = jax.random.uniform(jax.random.fold_in(jax.random.fold_in(stream_key, 6), axis_at), (blocks,), jnp.float32, smallest / len(cuts), largest / len(cuts))
        return jnp.repeat(jnp.exp(heights), shape[axis_at] // blocks).reshape((-1,) + (1,) * (len(shape) - axis_at - 1))

    factor_of = one(*cuts[0])
    for cut in cuts[1:]:
        factor_of = factor_of * one(*cut)
    return factor_of


def scatter_about(rng, shape, deviation, bound, cuts=(), kind=jnp.bfloat16):
    entries = deviation * jax.random.normal(rng, shape, jnp.float32)
    if cuts:
        entries = entries * block_levels(rng, shape, cuts, -0.22, 0.18)
    return jnp.clip(entries, -bound, bound).astype(kind)


def setup_inputs(seed: int = 0) -> dict:
    keys = jax.random.split(jax.random.key(seed), 12)
    return {
        "adjoint_u": scatter_about(keys[0], (NZ, NY, NX), 1.0, 6.0, ((0, 2), (1, 4), (2, 32)), jnp.float32),
        "adjoint_v": scatter_about(keys[1], (NZ, NY, NX), 1.0, 6.0, ((0, 2), (1, 4), (2, 32)), jnp.float32),
        "adjoint_t": scatter_about(keys[2], (NZ, NY, NX), 1.0, 6.0, ((0, 2), (1, 4), (2, 32)), jnp.float32),
        "zonal_vel": scatter_about(keys[3], (NZ, NY, NX), 0.3, 1.5, ((0, 2), (1, 4), (2, 32)), jnp.float32),
        "merid_vel": scatter_about(keys[4], (NZ, NY, NX), 0.3, 1.5, ((0, 2), (1, 4), (2, 32)), jnp.float32),
        "coriolis_dt": jnp.clip(jax.random.uniform(keys[5], (NY,), jnp.float32, -0.8, 0.8) * block_levels(keys[5], (NY,), ((0, 4),), -0.4, 0.0), -0.8, 0.8),
        "layer_thick": jnp.clip(jnp.exp(math.log(2.0) - 1.3862944 * jax.random.uniform(keys[6], (NZ,), jnp.float32) ** block_levels(keys[6], (NZ,), ((0, 2),), -0.2, 0.2)), 0.5, 2.0),
        "overturn_weight": jnp.clip(jnp.exp(math.log(3.0) - 2.3025851 * jax.random.uniform(keys[7], (NZ, NY), jnp.float32) ** block_levels(keys[7], (NZ, NY), ((1, 4),), -0.2, 0.2)), 0.3, 3.0),
        "overturn_target": scatter_about(keys[8], (NZ, NY), 1.0, 5.0, ((1, 4),), jnp.float32),
        "atlantic": draw_atlantic(jax.random.fold_in(keys[11], 71), 0),
        "bottom_level": plant(jax.random.randint(keys[10], (NY, NX), 0, NZ + 1), jax.random.fold_in(keys[10], 1), 0, NZ).astype(jnp.int32),
    }


press_coupling = 0.5

def take(padded, start, count, axis):
    return jax.lax.slice_in_dim(padded, start, start + count, axis=axis)

def fourth(padded, count, axis):
    near = take(padded, 3, count, axis) - take(padded, 1, count, axis)
    far = take(padded, 4, count, axis) - take(padded, 0, count, axis)
    return (8.0 * near - far) / 12.0

def second(padded, count, axis, width):
    return (take(padded, width + 1, count, axis) - take(padded, width - 1, count, axis)) / 2.0

def wrap_lon(field, width):
    return jnp.concatenate([field[:, :, -width:], field, field[:, :, :width]], axis=2)

def pad_lat(field, width):
    return jnp.pad(field, ((0, 0), (width, width), (0, 0)))

def reference(adjoint_u, adjoint_v, adjoint_t, zonal_vel, merid_vel, coriolis_dt, layer_thick, overturn_weight, overturn_target, atlantic, bottom_level):
    levels = jnp.arange(NZ, dtype=jnp.int32)[:, None, None]
    wet_cells = (levels < bottom_level[None]).astype(jnp.float32)
    basin = atlantic.astype(jnp.float32)[None]
    level_sum = lax.optimization_barrier(jnp.sum(basin * wet_cells * merid_vel, axis=2)) * layer_thick[:, None]
    suffix = jnp.flip(jnp.cumsum(jnp.flip(level_sum, 0), 0), 0)
    overturn = suffix / math.sqrt(NX * NZ)
    misfit = overturn_weight * (overturn - overturn_target)
    upward = jnp.cumsum(misfit, 0)
    cost_grad = basin * wet_cells * layer_thick[:, None, None] * upward[:, :, None] / math.sqrt(NZ)
    state_u = adjoint_u
    state_v = adjoint_v + cost_grad
    state_t = adjoint_t
    turning = coriolis_dt[None, :, None]
    for sweep_index in range(ITERS):
        masked_u = wet_cells * state_u
        masked_v = wet_cells * state_v
        masked_t = wet_cells * state_t
        tracer_x = fourth(wrap_lon(zonal_vel * masked_t, 2), NX, 2)
        tracer_y = fourth(pad_lat(merid_vel * masked_t, 2), NY, 1)
        press_x = second(wrap_lon(masked_u, 2), NX, 2, 2)
        press_y = second(pad_lat(masked_v, 2), NY, 1, 2)
        state_u = masked_u - turning * masked_v
        state_v = masked_v + turning * masked_u
        state_t = masked_t + tracer_x + tracer_y + press_coupling * (press_x + press_y)
    return (state_u, state_v, state_t)
```

```python
import jax
import jax.numpy as jnp
from jax import lax
from jax.experimental import pallas as pl
from jax.experimental.pallas import tpu as pltpu
from jax.sharding import PartitionSpec as P

MESH = pl.DeviceIdType.MESH
F32 = jnp.float32
HALO = 8
OWN = 32
ROWS = OWN + 2 * HALO
NLON, NLAT, NDEP = 32, 4, 2
RING_Y, RING_Z = 4, 8
T, V, VV, UU, U = range(5)


def lanes():
    return lax.broadcasted_iota(jnp.int32, (8, 128), 1)


def sublanes():
    return lax.broadcasted_iota(jnp.int32, (8, 128), 0)


def lroll(x, shift):
    shift = shift % 128
    return x if shift == 0 else pltpu.roll(x, shift, 1)


def sroll(x, shift):
    return pltpu.roll(x, shift % 8, 0)


def pack(tiles):
    at = (lanes() + 8) // 32 % 4
    joined = tiles[0]
    for g in range(1, 4):
        joined = jnp.where(at == g, lroll(tiles[g], 32 * g), joined)
    return jnp.where(lanes() % 32 < 16, lroll(joined, 8), lroll(joined, 24))


def merge(own, left, right):
    place = lanes() % 32
    return jnp.where(
        place < 8, lroll(left, -16), jnp.where(place >= 24, lroll(right, 16), own)
    )


def spread(strip):
    return jnp.where(lanes() % 32 < 16, lroll(strip, -8), lroll(strip, -24))


def suffix_tile(x):
    lane, sub = lanes(), sublanes()
    for k in (1, 2, 4):
        x = x + jnp.where(sub < 8 - k, sroll(x, -k), 0.0)
    group = jnp.broadcast_to(x[0:1, :], (8, 128))
    out, total = x, group
    for j in (1, 2, 3):
        moved = lroll(group, -32 * j)
        out = out + jnp.where(lane < 128 - 32 * j, moved, 0.0)
        total = total + moved
    return out, total


def prefix_tile(x):
    lane, sub = lanes(), sublanes()
    for k in (1, 2, 4):
        x = x + jnp.where(sub >= k, sroll(x, k), 0.0)
    group = jnp.broadcast_to(x[7:8, :], (8, 128))
    out, total = x, group
    for j in (1, 2, 3):
        moved = lroll(group, 32 * j)
        out = out + jnp.where(lane >= 32 * j, moved, 0.0)
        total = total + moved
    return out, total


def by_rows(low, high, block, fn):
    def body(n, c):
        stores = []
        for r in range(block):
            stores += fn(low + block * n + r)
        for ref, index, value in stores:
            ref[index] = value
        return c

    lax.fori_loop(0, (high - low) // block, body, 0)


def reduce_lanes(make):
    lane = lanes()

    def tree(level, start):
        if level < 0:
            return make(start)
        step = 1 << level
        a = tree(level - 1, start)
        b = tree(level - 1, start + step)
        even = (lane & step) == 0
        return jnp.where(even, a, b) + lroll(jnp.where(even, b, a), -step)

    return tree(6, 0)


def kernel(
    adj_u, adj_v, adj_t, zonal, merid, cor, thick, weight_t, target_t, atl, bottom,
    out_u, out_v, out_t,
    raw, tr, uu, vv, mask, strips_own, strips_l, strips_r, s_raw, s_mask, s_tr, s_edge,
    flat, coef, flat_own, flat_l, flat_r, flat_s, ints, wt, cor_s, thick_s,
    a_src, a_dst, b_src, b_dst, y_dst, o_src, l_dst, r_dst, res,
    load_sem, small_sem, a_ss, a_rs, b_ss, b_rs, h_ss, h_rs, m_ss, m_rs, out_sem,
):
    lon, lat, dep = lax.axis_index("lon"), lax.axis_index("lat"), lax.axis_index("dep")
    ring_y, ring_z = lon % RING_Y, lon // RING_Y

    sources = (adj_t, merid, adj_v, adj_u, zonal)
    for i in (V, T, VV, UU, U):
        def load(z, c, i=i):
            pltpu.make_async_copy(
                sources[i].at[z], raw.at[i, pl.ds(HALO, OWN), z], load_sem.at[i]
            ).start()
            return c
        if i == V:
            smalls = [
                pltpu.make_async_copy(bottom, ints.at[0], small_sem.at[0]),
                pltpu.make_async_copy(atl, ints.at[1], small_sem.at[1]),
                pltpu.make_async_copy(weight_t, wt.at[0], small_sem.at[2]),
                pltpu.make_async_copy(target_t, wt.at[1], small_sem.at[3]),
                pltpu.make_async_copy(cor, cor_s, small_sem.at[4]),
                pltpu.make_async_copy(thick, thick_s, small_sem.at[5]),
            ]
            for copy in smalls:
                copy.start()
        lax.fori_loop(0, OWN, load, 0)

    def wait_load(i):
        pltpu.make_async_copy(
            sources[i], raw.at[i, pl.ds(HALO, OWN)], load_sem.at[i]
        ).wait()

    def wrap(i, n):
        return lax.rem(i + n, n)

    def ring_y_peer(k):
        return ring_z * RING_Y + lax.rem(ring_y + k, RING_Y)

    right, left = wrap(lon + 1, NLON), wrap(lon - 1, NLON)
    above, below = wrap(lat - 1, NLAT), wrap(lat + 1, NLAT)
    first_stage = []
    for slab, to_lat in ((0, lat), (1, below), (2, above)):
        for k in range(RING_Y):
            for d in range(NDEP):
                if slab == 0 and k == 0 and d == 0:
                    continue
                to_dep = dep if d == 0 else 1 - dep
                first_stage.append((slab, 2 * k + d, d, (ring_y_peer(k), to_lat, to_dep)))
    second_stage = [
        (k, (lax.rem(lon + RING_Y * k, NLON), lat, dep)) for k in range(1, RING_Z)
    ]
    around = [
        (right, lat, dep), (left, lat, dep),
        (right, above, dep), (left, above, dep), (right, below, dep), (left, below, dep),
    ]
    barrier = pltpu.get_barrier_semaphore()
    greeted = [p[3] for p in first_stage] + [p[1] for p in second_stage] + around
    for peer in greeted:
        pl.semaphore_signal(barrier, inc=1, device_id=peer, device_id_type=MESH)

    lane, sub = lanes(), sublanes()
    for copy in smalls:
        copy.wait()
    for y in range(0, OWN, 8):
        flat[0, pl.ds(HALO + y, 8)] = ints[0, pl.ds(y, 8)].astype(F32)
        flat[1, pl.ds(HALO + y, 8)] = ints[1, pl.ds(y, 8)].astype(F32)
        turning = jnp.zeros((8, 128), F32)
        for r in range(8):
            turning = jnp.where(sub == r, cor_s[y + r], turning)
        flat[2, pl.ds(HALO + y, 8)] = turning
    thickness = jnp.zeros((8, 128), F32)
    for z in range(OWN):
        here = jnp.logical_and(sub == z % 8, lane // 32 == z // 8)
        thickness = jnp.where(here, thick_s[z], thickness)

    depth_main = [(dep * OWN + 8 * g + sub).astype(F32) for g in range(4)]
    depth_strip = (dep * OWN + 8 * (lane // 32) + sub).astype(F32)

    def row(ref, i, y):
        return jnp.broadcast_to(ref[i, pl.ds(y, 1), :], (8, 128))

    wait_load(V)

    def basin_flow(i):
        g, y = i // OWN, HALO + i % OWN
        inside = depth_main[g] < row(flat, 0, y)
        return jnp.where(inside, raw[V, y, pl.ds(8 * g, 8), :], 0.0) * row(flat, 1, y)

    level_sum = reduce_lanes(basin_flow) * thickness

    def packed(i):
        filled = jnp.concatenate([wt[i], jnp.zeros((32, 64), F32)], axis=1)
        filled = jnp.concatenate([filled, jnp.zeros((96, 128), F32)], axis=0)
        turned = filled.T
        halves = []
        for half in range(2):
            tile = turned[32 * half:32 * half + 8]
            for g in range(1, 4):
                start = 32 * half + 8 * g
                tile = jnp.where(lane // 32 == g, lroll(turned[start:start + 8], 32 * g), tile)
            halves.append(tile)
        lower = dep == 1
        return jnp.where(lower, halves[1], halves[0]), jnp.where(lower, halves[0], halves[1])

    w_own, w_other = packed(0)
    g_own, g_other = packed(1)
    deeper, whole = suffix_tile(level_sum)
    is_low = jnp.where(dep == 1, 1.0, 0.0)
    mis_own = w_own * (deeper * (1.0 / 512.0) - g_own * (1.0 / 64.0))
    mis_other = w_other * (whole * is_low * (1.0 / 512.0) - g_other * (1.0 / 64.0))
    up_own, tot_own = prefix_tile(mis_own)
    up_other, tot_other = prefix_tile(mis_other)
    a_src[0] = up_own + is_low * tot_other
    a_src[1] = up_other + (1.0 - is_low) * tot_own

    pl.semaphore_wait(barrier, len(greeted))

    def send(src, dst, ss, rs, peer):
        copy = pltpu.make_async_remote_copy(
            src_ref=src, dst_ref=dst, send_sem=ss, recv_sem=rs,
            device_id=peer, device_id_type=MESH,
        )
        copy.start()
        return copy

    a_copies = [
        send(a_src.at[d], a_dst.at[slab, slot], a_ss.at[8 * slab + slot], a_rs.at[8 * slab + slot], peer)
        for slab, slot, d, peer in first_stage
    ]

    h_copies = []

    def halo_send(src, dst, peer):
        n = len(h_copies)
        h_copies.append(send(src, dst, h_ss.at[n], h_rs.at[n], peer))

    low, high = pl.ds(HALO, HALO), pl.ds(OWN, HALO)
    top, end = pl.ds(0, HALO), pl.ds(HALO + OWN, HALO)
    halo_send(flat.at[:, low], flat.at[:, end], (lon, above, dep))
    halo_send(flat.at[:, high], flat.at[:, top], (lon, below, dep))
    wait_load(T)
    wait_load(VV)
    wait_load(UU)
    wait_load(U)
    four_raw = pl.ds(0, 4)
    halo_send(raw.at[four_raw, low], raw.at[four_raw, end], (lon, above, dep))
    halo_send(raw.at[four_raw, high], raw.at[four_raw, top], (lon, below, dep))
    halo_send(raw.at[U, pl.ds(HALO, 6)], raw.at[U, pl.ds(HALO + OWN, 6)], (lon, above, dep))
    halo_send(raw.at[U, pl.ds(OWN + 2, 6)], raw.at[U, pl.ds(2, 6)], (lon, below, dep))

    for i in range(2):
        for y in range(0, OWN, 8):
            tile = flat[i, pl.ds(HALO + y, 8), :]
            flat_own[i, pl.ds(y, 8), :] = pack([tile] * 4)

    def pack_row(y):
        return [
            (strips_own, (i, y), pack([raw[i, HALO + y, pl.ds(8 * g, 8), :] for g in range(4)]))
            for i in range(5)
        ]

    by_rows(0, OWN, 4, pack_row)

    def strip_sends(put, src, dst_l, dst_r, own_lead):
        body, first, last = pl.ds(HALO, OWN), pl.ds(0, HALO), pl.ds(OWN - HALO, HALO)
        sl = (slice(None),) if own_lead else ()
        put(src, dst_l.at[sl + (body,)], (right, lat, dep))
        put(src, dst_r.at[sl + (body,)], (left, lat, dep))
        put(src.at[sl + (first,)], dst_l.at[sl + (end,)], (right, above, dep))
        put(src.at[sl + (first,)], dst_r.at[sl + (end,)], (left, above, dep))
        put(src.at[sl + (last,)], dst_l.at[sl + (top,)], (right, below, dep))
        put(src.at[sl + (last,)], dst_r.at[sl + (top,)], (left, below, dep))

    strip_sends(halo_send, flat_own, flat_l, flat_r, True)
    strip_sends(halo_send, strips_own, strips_l, strips_r, True)

    for copy in a_copies:
        copy.wait()
    a_dst[0, 0] = a_src[0]
    sums = []
    for slab in range(3):
        total = a_dst[slab, 0]
        for k in range(1, 8):
            total = total + a_dst[slab, k]
        sums.append(total)
    b_src[0] = sums[0]
    b_src[1] = jnp.where(lane % 32 >= 16, sums[1], sums[2])
    b_copies = [
        send(b_src, b_dst.at[k], b_ss.at[k], b_rs.at[k], peer) for k, peer in second_stage
    ]

    def prepare_row(y):
        deep = row(flat, 0, y)
        stores = []
        for g in range(4):
            at = pl.ds(8 * g, 8)
            inside = depth_main[g] < deep
            stores += [
                (mask, (y, at), jnp.where(inside, 1.0 / 12.0, 0.0)),
                (tr, (0, y, at), jnp.where(inside, raw[T, y, at, :], 0.0)),
                (uu, (y, at), jnp.where(inside, 3.0 * raw[UU, y, at, :], 0.0)),
            ]
        return stores

    by_rows(HALO, HALO + OWN, 4, prepare_row)

    for copy in h_copies:
        copy.wait()
    has_above = jnp.where(lat > 0, 1.0, 0.0)
    has_below = jnp.where(lat < NLAT - 1, 1.0, 0.0)
    flat[0, top] = flat[0, top] * has_above
    flat[0, end] = flat[0, end] * has_below
    by_rows(0, HALO, 4, prepare_row)
    by_rows(HALO + OWN, ROWS, 4, prepare_row)
    for y in range(0, ROWS, 8):
        at = pl.ds(y, 8)
        turning = flat[2, at]
        real, imag = jnp.ones((8, 128), F32), jnp.zeros((8, 128), F32)
        for k in range(9):
            coef[2 * k, at] = real
            coef[2 * k + 1, at] = imag
            real, imag = real - turning * imag, imag + turning * real
    for i in range(2):
        for y in range(0, ROWS, 8):
            at = pl.ds(y, 8)
            own = pack([flat[i, at, :]] * 4)
            flat_s[i, at, :] = merge(own, flat_l[i, at, :], flat_r[i, at, :])
    flat_s[0, top] = flat_s[0, top] * has_above
    flat_s[0, end] = flat_s[0, end] * has_below

    def strip_row(y, own):
        inside = depth_strip < row(flat_s, 0, y)
        stores = [(s_mask, y, jnp.where(inside, 1.0 / 12.0, 0.0))]
        for i in range(5):
            tile = merge(own(i), strips_l[i, y], strips_r[i, y])
            if i == T:
                stores.append((s_tr, (0, y), jnp.where(inside, tile, 0.0)))
                continue
            if i == UU:
                tile = jnp.where(inside, 3.0 * tile, 0.0)
            stores.append((s_raw, (i, y), tile))
        return stores

    by_rows(HALO, HALO + OWN, 4, lambda y: strip_row(y, lambda i: strips_own[i, y - HALO]))
    raw[U, pl.ds(0, 2)] = jnp.zeros((2, 32, 128), F32)
    raw[U, pl.ds(ROWS - 2, 2)] = jnp.zeros((2, 32, 128), F32)

    def strip_outer(y):
        return strip_row(
            y, lambda i: pack([raw[i, y, pl.ds(8 * g, 8), :] for g in range(4)])
        )

    by_rows(0, HALO, 4, strip_outer)
    by_rows(HALO + OWN, ROWS, 4, strip_outer)

    for copy in b_copies:
        copy.wait()
    ups = []
    for i in range(2):
        total = b_src[i]
        for k in range(1, RING_Z):
            total = total + b_dst[k, i]
        ups.append(total * thickness * 4.5)

    def gradient(y, up, offset):
        moved = pltpu.roll(up, lax.rem(256 + offset - y, 128), 1)
        spreads = [jnp.broadcast_to(moved[:, 32 * g:32 * g + 1], (8, 128)) for g in range(4)]
        basin = row(flat, 1, y)
        stores = []
        for g in range(4):
            at = pl.ds(8 * g, 8)
            value = mask[y, at, :] * (36.0 * raw[VV, y, at, :] + basin * spreads[g])
            stores.append((vv, (y, at), value))
        joined = spreads[0]
        for g in range(1, 4):
            joined = jnp.where(lane // 32 == g, spreads[g], joined)
        value = s_mask[y] * (36.0 * s_raw[VV, y] + row(flat_s, 1, y) * joined)
        stores.append((s_raw, (VV, y), value))
        return stores

    by_rows(HALO, HALO + OWN, 4, lambda y: gradient(y, ups[0], HALO))
    by_rows(0, HALO, 4, lambda y: gradient(y, ups[1], HALO - OWN))
    by_rows(HALO + OWN, ROWS, 4, lambda y: gradient(y, ups[1], HALO + OWN))

    edge = jnp.logical_or(lane < 2, lane >= 126)

    def column(k, first, last, get, emit):
        rows = range(first, ROWS - first)
        flux, held, us, vs = {}, {}, {}, {}

        def reach(y):
            held[y] = get("t", y)
            flux[y] = get("V", y) * held[y]

        def turn(y):
            u_0, v_0 = get("u", y), get("v", y)
            if k == 0:
                us[y], vs[y] = u_0, v_0
            else:
                real, imag = row(coef, 2 * k, y), row(coef, 2 * k + 1, y)
                us[y], vs[y] = real * u_0 - imag * v_0, real * v_0 + imag * u_0

        for y in range(first - 2, first + 2):
            reach(y)
        for y in (first - 1, first):
            turn(y)
        for y in rows:
            reach(y + 2)
            turn(y + 1)
            q_x = get("U", y) * held[y]
            a_x = 8.0 * q_x + us[y]
            z_x = (lroll(a_x, -1) - lroll(a_x, 1)) - (lroll(q_x, -2) - lroll(q_x, 2))
            z_y = 8.0 * (flux[y + 1] - flux[y - 1]) + (vs[y + 1] - vs[y - 1])
            z_y = z_y - (flux[y + 2] - flux[y - 2])
            scale = (1.0 / 12.0) if last else get("m", y)
            emit(y, held[y] + scale * (z_x + z_y))

    def step(k, first, last=False):
        now, new = k % 2, 1 - k % 2

        def strip_get(what, y):
            return {
                "t": lambda: s_tr[now, y], "u": lambda: s_raw[UU, y], "v": lambda: s_raw[VV, y],
                "m": lambda: s_mask[y], "U": lambda: s_raw[U, y], "V": lambda: s_raw[V, y],
            }[what]()

        def strip_emit(y, value):
            s_tr[new, y] = value
            s_edge[y] = spread(value)

        column(k, first, last, strip_get, strip_emit)

        def group(g, c):
            at = pl.ds(pl.multiple_of(8 * g, 8), 8)

            def get(what, y):
                return {
                    "t": lambda: tr[now, y, at, :], "u": lambda: uu[y, at, :],
                    "v": lambda: vv[y, at, :], "m": lambda: mask[y, at, :],
                    "U": lambda: raw[U, y, at, :], "V": lambda: raw[V, y, at, :],
                }[what]()

            def emit(y, value):
                fixed = pltpu.roll(s_edge[y], lax.rem(128 - 32 * g, 128), 1)
                tr[new, y, at, :] = jnp.where(edge, fixed, value)

            column(k, first, last, get, emit)
            return c

        lax.fori_loop(0, 4, group, 0)

    def refresh(y):
        own = pack([tr[0, y, pl.ds(8 * g, 8), :] for g in range(4)])
        place = lane % 32
        keep = jnp.logical_or(place < 8, place >= 24)
        return [(s_tr, (0, y), jnp.where(keep, s_tr[0, y], own))]

    def four(k, last=False):
        step(k, 2)
        step(k + 1, 4)
        by_rows(4, ROWS - 4, 8, refresh)
        step(k + 2, 6)
        step(k + 3, 8, last)

    four(0)

    m_copies = []

    def mid_send(src, dst, peer):
        n = len(m_copies)
        m_copies.append(send(src, dst, m_ss.at[n], m_rs.at[n], peer))

    mid_send(tr.at[0, low], y_dst.at[1], (lon, above, dep))
    mid_send(tr.at[0, high], y_dst.at[0], (lon, below, dep))

    def pack_tracer(y):
        return [(o_src, y, pack([tr[0, HALO + y, pl.ds(8 * g, 8), :] for g in range(4)]))]

    by_rows(0, OWN, 8, pack_tracer)
    strip_sends(mid_send, o_src, l_dst, r_dst, False)

    def turned(y):
        stores = []
        real, imag = row(coef, 16, y) * (1.0 / 3.0), row(coef, 17, y) * (1.0 / 3.0)
        for g in range(4):
            at = pl.ds(8 * g, 8)
            u_0, v_0 = uu[y, at, :], vv[y, at, :]
            stores.append((res, (0, y - HALO, at), real * u_0 - imag * v_0))
            stores.append((res, (1, y - HALO, at), real * v_0 + imag * u_0))
        return stores

    by_rows(HALO, HALO + OWN, 4, turned)

    def store_out(n, held, out):
        def store(z, c):
            pltpu.make_async_copy(held.at[:, z], out.at[z], out_sem.at[n]).start()
            return c
        lax.fori_loop(0, OWN, store, 0)

    store_out(0, res.at[0], out_u)
    store_out(1, res.at[1], out_v)

    for copy in m_copies:
        copy.wait()

    def halo_row(y):
        stores = []
        for n, at, valid in ((0, y, has_above), (1, HALO + OWN + y, has_below)):
            tiles = [y_dst[n, y, pl.ds(8 * g, 8), :] * valid for g in range(4)]
            stores += [(tr, (0, at, pl.ds(8 * g, 8)), tiles[g]) for g in range(4)]
            stores.append((s_tr, (0, at), merge(pack(tiles), l_dst[at] * valid, r_dst[at] * valid)))
        return stores

    by_rows(0, HALO, 4, halo_row)
    by_rows(
        HALO, HALO + OWN, 8,
        lambda y: [(s_tr, (0, y), merge(o_src[y - HALO], l_dst[y], r_dst[y]))],
    )
    four(4, True)

    result = tr.at[0, pl.ds(HALO, OWN)]
    store_out(2, result, out_t)
    for n, (held, out) in enumerate(((res.at[0], out_u), (res.at[1], out_v), (result, out_t))):
        pltpu.make_async_copy(held, out, out_sem.at[n]).wait()


def per_device(*args):
    args = args[:7] + (args[7].T, args[8].T) + args[9:]
    block = jax.ShapeDtypeStruct((32, 32, 128), F32)
    main = pltpu.VMEM((ROWS, 32, 128), F32)
    strip = pltpu.VMEM((ROWS, 8, 128), F32)
    dma = pltpu.SemaphoreType.DMA
    return pl.pallas_call(
        kernel,
        out_shape=(block,) * 3,
        in_specs=[pl.BlockSpec(memory_space=pltpu.HBM)] * 11,
        out_specs=(pl.BlockSpec(memory_space=pltpu.HBM),) * 3,
        scratch_shapes=[
            pltpu.VMEM((5, ROWS, 32, 128), F32),
            pltpu.VMEM((2, ROWS, 32, 128), F32),
            main, main, main,
            pltpu.VMEM((5, OWN, 8, 128), F32),
            pltpu.VMEM((5, ROWS, 8, 128), F32),
            pltpu.VMEM((5, ROWS, 8, 128), F32),
            pltpu.VMEM((5, ROWS, 8, 128), F32),
            strip,
            pltpu.VMEM((2, ROWS, 8, 128), F32),
            strip,
            pltpu.VMEM((3, ROWS, 128), F32),
            pltpu.VMEM((18, ROWS, 128), F32),
            pltpu.VMEM((2, OWN, 128), F32),
            pltpu.VMEM((2, ROWS, 128), F32),
            pltpu.VMEM((2, ROWS, 128), F32),
            pltpu.VMEM((2, ROWS, 128), F32),
            pltpu.VMEM((2, OWN, 128), jnp.int32),
            pltpu.VMEM((2, 32, 64), F32),
            pltpu.SMEM((32,), F32),
            pltpu.SMEM((32,), F32),
            pltpu.VMEM((2, 8, 128), F32),
            pltpu.VMEM((3, 8, 8, 128), F32),
            pltpu.VMEM((2, 8, 128), F32),
            pltpu.VMEM((8, 2, 8, 128), F32),
            pltpu.VMEM((2, HALO, 32, 128), F32),
            pltpu.VMEM((OWN, 8, 128), F32),
            strip, strip,
            pltpu.VMEM((2, OWN, 32, 128), F32),
            dma((5,)), dma((6,)), dma((24,)), dma((24,)), dma((8,)), dma((8,)),
            dma((18,)), dma((18,)), dma((8,)), dma((8,)), dma((3,)),
        ],
        compiler_params=pltpu.CompilerParams(
            collective_id=0, has_side_effects=True, vmem_limit_bytes=60 * 1024 * 1024
        ),
        name="adjoint",
    )(*args)


def solution(mesh):
    block, level = P("dep", "lat", "lon"), P(None, "lat")
    in_specs = (block,) * 5 + (P("lat"), P("dep"), level, level) + (P("lat", "lon"),) * 2
    return jax.shard_map(
        per_device, mesh=mesh, in_specs=in_specs, out_specs=(block,) * 3, check_vma=False
    )
```

```python
import jax
import jax.numpy as jnp
from jax import lax
from jax.experimental import pallas as pl
from jax.experimental.pallas import tpu as pltpu
from jax.sharding import PartitionSpec as P

MESH = pl.DeviceIdType.MESH
F32 = jnp.float32
BF16 = jnp.bfloat16
HALO = 8
OWN = 32
ROWS = OWN + 2 * HALO
NLON, NLAT, NDEP = 32, 4, 2
RING_Y, RING_Z = 4, 8
T, V, VV, UU, U = range(5)


def lanes():
    return lax.broadcasted_iota(jnp.int32, (8, 128), 1)


def sublanes():
    return lax.broadcasted_iota(jnp.int32, (8, 128), 0)


def lroll(x, shift):
    shift = shift % 128
    return x if shift == 0 else pltpu.roll(x, shift, 1)


def sroll(x, shift):
    return pltpu.roll(x, shift % 8, 0)


def pack(tiles):
    at = (lanes() + 8) // 32 % 4
    joined = tiles[0]
    for g in range(1, 4):
        joined = jnp.where(at == g, lroll(tiles[g], 32 * g), joined)
    return jnp.where(lanes() % 32 < 16, lroll(joined, 8), lroll(joined, 24))


def merge(own, left, right, slot=2, other=1):
    place = lanes() % 32
    return jnp.where(
        place < 8,
        lroll(left, -8 * slot),
        jnp.where(place >= 24, lroll(right, 24 - 8 * other), own),
    )


def pack_four(strips):
    at = lanes() // 8 % 4
    both = []
    for base in (16, 8):
        joined = lroll(strips[0], -base)
        for j in range(1, 4):
            joined = jnp.where(at == j, lroll(strips[j], 8 * j - base), joined)
        both.append(joined)
    return both


def slope_matrix(kind, group):
    i = lax.broadcasted_iota(jnp.int32, (128, 128), 0)
    j = lax.broadcasted_iota(jnp.int32, (128, 128), 1)
    if group is not None:
        place = i % 32
        halo = jnp.logical_or(place < 8, place >= 24)
        here = jnp.logical_and(halo, i // 32 == group)
        i = jnp.where(here, jnp.where(place < 8, place - 8, place + 104), 1000)
    apart = i - j
    near, far = (8.0, 1.0) if kind == 0 else (1.0, 0.0)
    out = jnp.where(apart == 1, near, jnp.where(apart == -1, -near, 0.0))
    return out + jnp.where(apart == 2, -far, jnp.where(apart == -2, far, 0.0))


def split(x):
    high = x.astype(BF16)
    return jnp.concatenate([high, (x - high.astype(F32)).astype(BF16)], axis=1)


def suffix_tile(x):
    lane, sub = lanes(), sublanes()
    for k in (1, 2, 4):
        x = x + jnp.where(sub < 8 - k, sroll(x, -k), 0.0)
    group = jnp.broadcast_to(x[0:1, :], (8, 128))
    out, total = x, group
    for j in (1, 2, 3):
        moved = lroll(group, -32 * j)
        out = out + jnp.where(lane < 128 - 32 * j, moved, 0.0)
        total = total + moved
    return out, total


def prefix_tile(x):
    lane, sub = lanes(), sublanes()
    for k in (1, 2, 4):
        x = x + jnp.where(sub >= k, sroll(x, k), 0.0)
    group = jnp.broadcast_to(x[7:8, :], (8, 128))
    out, total = x, group
    for j in (1, 2, 3):
        moved = lroll(group, 32 * j)
        out = out + jnp.where(lane >= 32 * j, moved, 0.0)
        total = total + moved
    return out, total


def by_rows(low, high, block, fn):
    def body(n, c):
        stores = []
        for r in range(block):
            stores += fn(low + block * n + r)
        for ref, index, value in stores:
            ref[index] = value
        return c

    lax.fori_loop(0, (high - low) // block, body, 0)


def reduce_lanes(make):
    lane = lanes()

    def tree(level, start):
        if level < 0:
            return make(start)
        step = 1 << level
        a = tree(level - 1, start)
        b = tree(level - 1, start + step)
        even = (lane & step) == 0
        return jnp.where(even, a, b) + lroll(jnp.where(even, b, a), -step)

    return tree(6, 0)


def kernel(
    adj_u, adj_v, adj_t, zonal, merid, cor, thick, weight_t, target_t, atl, bottom,
    out_u, out_v, out_t,
    raw, tr, uu, vv, mask, strips_own, strips_send, strips_l, strips_r, s_raw, s_mask, s_tr,
    zx, corr, xu, xv, xb, s_xu, s_xv, s_xb, main_mat, strip_mat,
    flat, coef, flat_own, flat_l, flat_r, flat_s, ints, wt, cor_s, thick_s,
    a_src, a_dst, b_src, b_dst, y_src, y_dst, o_src, o_send, l_dst, r_dst, res,
    load_sem, small_sem, a_ss, a_rs, b_ss, b_rs, h_ss, h_rs, m_ss, m_rs, out_sem,
):
    lon, lat, dep = lax.axis_index("lon"), lax.axis_index("lat"), lax.axis_index("dep")
    ring_y, ring_z = lon % RING_Y, lon // RING_Y

    sources = (adj_t, merid, adj_v, adj_u, zonal)
    for i in (V, T, VV, UU, U):
        def load(z, c, i=i):
            pltpu.make_async_copy(
                sources[i].at[z], raw.at[i, pl.ds(HALO, OWN), z], load_sem.at[i]
            ).start()
            return c
        if i == V:
            smalls = [
                pltpu.make_async_copy(bottom, ints.at[0], small_sem.at[0]),
                pltpu.make_async_copy(atl, ints.at[1], small_sem.at[1]),
                pltpu.make_async_copy(weight_t, wt.at[0], small_sem.at[2]),
                pltpu.make_async_copy(target_t, wt.at[1], small_sem.at[3]),
                pltpu.make_async_copy(cor, cor_s, small_sem.at[4]),
                pltpu.make_async_copy(thick, thick_s, small_sem.at[5]),
            ]
            for copy in smalls:
                copy.start()
        lax.fori_loop(0, OWN, load, 0)

    def wait_load(i):
        pltpu.make_async_copy(
            sources[i], raw.at[i, pl.ds(HALO, OWN)], load_sem.at[i]
        ).wait()

    def wrap(i, n):
        return lax.rem(i + n, n)

    def ring_y_peer(k):
        return ring_z * RING_Y + lax.rem(ring_y + k, RING_Y)

    right, left = wrap(lon + 1, NLON), wrap(lon - 1, NLON)
    above, below = wrap(lat - 1, NLAT), wrap(lat + 1, NLAT)
    first_stage = []
    for slab, to_lat in ((0, lat), (1, below), (2, above)):
        for k in range(RING_Y):
            for d in range(NDEP):
                if slab == 0 and k == 0 and d == 0:
                    continue
                to_dep = dep if d == 0 else 1 - dep
                first_stage.append((slab, 2 * k + d, d, (ring_y_peer(k), to_lat, to_dep)))
    second_stage = [
        (k, (lax.rem(lon + RING_Y * k, NLON), lat, dep)) for k in range(1, RING_Z)
    ]
    around = [
        (right, lat, dep), (left, lat, dep),
        (right, above, dep), (left, above, dep), (right, below, dep), (left, below, dep),
    ]
    barrier = pltpu.get_barrier_semaphore()
    greeted = [p[3] for p in first_stage] + [p[1] for p in second_stage] + around
    for peer in greeted:
        pl.semaphore_signal(barrier, inc=1, device_id=peer, device_id_type=MESH)

    lane, sub = lanes(), sublanes()
    for copy in smalls:
        copy.wait()
    for y in range(0, OWN, 8):
        flat[0, pl.ds(HALO + y, 8)] = ints[0, pl.ds(y, 8)].astype(F32)
        flat[1, pl.ds(HALO + y, 8)] = ints[1, pl.ds(y, 8)].astype(F32)
        turning = jnp.zeros((8, 128), F32)
        for r in range(8):
            turning = jnp.where(sub == r, cor_s[y + r], turning)
        flat[2, pl.ds(HALO + y, 8)] = turning
    thickness = jnp.zeros((8, 128), F32)
    for z in range(OWN):
        here = jnp.logical_and(sub == z % 8, lane // 32 == z // 8)
        thickness = jnp.where(here, thick_s[z], thickness)

    for kind in range(2):
        for n in range(5):
            mat = slope_matrix(kind, None if n == 0 else n - 1).astype(BF16)
            for half in range(2):
                strip_mat[kind, pl.ds(128 * half, 128), pl.ds(128 * n, 128)] = mat
                if n == 0:
                    main_mat[kind, pl.ds(128 * half, 128), :] = mat

    depth_main = [(dep * OWN + 8 * g + sub).astype(F32) for g in range(4)]
    depth_strip = (dep * OWN + 8 * (lane // 32) + sub).astype(F32)

    def row(ref, i, y):
        return jnp.broadcast_to(ref[i, pl.ds(y, 1), :], (8, 128))

    wait_load(V)

    def basin_flow(i):
        g, y = i // OWN, HALO + i % OWN
        inside = depth_main[g] < row(flat, 0, y)
        return jnp.where(inside, raw[V, y, pl.ds(8 * g, 8), :], 0.0) * row(flat, 1, y)

    level_sum = reduce_lanes(basin_flow) * thickness

    def packed(i):
        filled = jnp.concatenate([wt[i], jnp.zeros((32, 64), F32)], axis=1)
        filled = jnp.concatenate([filled, jnp.zeros((96, 128), F32)], axis=0)
        turned = filled.T
        halves = []
        for half in range(2):
            tile = turned[32 * half:32 * half + 8]
            for g in range(1, 4):
                start = 32 * half + 8 * g
                tile = jnp.where(lane // 32 == g, lroll(turned[start:start + 8], 32 * g), tile)
            halves.append(tile)
        lower = dep == 1
        return jnp.where(lower, halves[1], halves[0]), jnp.where(lower, halves[0], halves[1])

    w_own, w_other = packed(0)
    g_own, g_other = packed(1)
    deeper, whole = suffix_tile(level_sum)
    is_low = jnp.where(dep == 1, 1.0, 0.0)
    mis_own = w_own * (deeper * (1.0 / 512.0) - g_own * (1.0 / 64.0))
    mis_other = w_other * (whole * is_low * (1.0 / 512.0) - g_other * (1.0 / 64.0))
    up_own, tot_own = prefix_tile(mis_own)
    up_other, tot_other = prefix_tile(mis_other)
    a_src[0] = up_own + is_low * tot_other
    a_src[1] = up_other + (1.0 - is_low) * tot_own

    def clear(rows, tiles, few, side, slab):
        raw[:, rows] = jnp.zeros((5, HALO, 32, 128), F32)
        flat[:, rows] = jnp.zeros((3, HALO, 128), F32)
        a_dst[slab] = jnp.zeros((8, 8, 128), F32)
        y_dst[side] = jnp.zeros((HALO, 32, 128), F32)
        for ref in (strips_l, strips_r):
            ref[tiles] = jnp.zeros((10, 8, 128), F32)
        for ref in (flat_l, flat_r):
            ref[:, rows] = jnp.zeros((2, HALO, 128), F32)
        for ref in (l_dst, r_dst):
            ref[few] = jnp.zeros((2, 8, 128), F32)

    @pl.when(lat == 0)
    def _():
        clear(pl.ds(0, HALO), pl.ds(0, 10), pl.ds(0, 2), 0, 1)

    @pl.when(lat == NLAT - 1)
    def _():
        clear(pl.ds(HALO + OWN, HALO), pl.ds(50, 10), pl.ds(10, 2), 1, 2)

    pl.semaphore_wait(barrier, len(greeted))

    inner = {-1: lat > 0, 1: lat < NLAT - 1}

    def when(condition, act):
        if condition is None:
            act()
        else:
            pl.when(condition)(act)

    def send(src, dst, ss, rs, peer, toward=0):
        copy = pltpu.make_async_remote_copy(
            src_ref=src, dst_ref=dst, send_sem=ss, recv_sem=rs,
            device_id=peer, device_id_type=MESH,
        )
        when(inner.get(toward), copy.start)
        return copy, toward

    def finish(copies):
        for copy, toward in copies:
            when(inner.get(-toward), copy.wait_recv)
        for copy, toward in copies:
            when(inner.get(toward), copy.wait_send)

    a_copies = [
        send(a_src.at[d], a_dst.at[slab, slot], a_ss.at[8 * slab + slot], a_rs.at[8 * slab + slot], peer, (0, 1, -1)[slab])
        for slab, slot, d, peer in first_stage
    ]

    h_copies = []

    def halo_send(src, dst, peer, toward=0):
        n = len(h_copies)
        h_copies.append(send(src, dst, h_ss.at[n], h_rs.at[n], peer, toward))

    low, high = pl.ds(HALO, HALO), pl.ds(OWN, HALO)
    top, end = pl.ds(0, HALO), pl.ds(HALO + OWN, HALO)
    halo_send(flat.at[:, low], flat.at[:, end], (lon, above, dep), -1)
    halo_send(flat.at[:, high], flat.at[:, top], (lon, below, dep), 1)
    for i in range(2):
        for y in range(0, OWN, 8):
            tile = flat[i, pl.ds(HALO + y, 8), :]
            flat_own[i, pl.ds(y, 8), :] = pack([tile] * 4)

    def flat_sends():
        body, first, last = pl.ds(HALO, OWN), pl.ds(0, HALO), pl.ds(OWN - HALO, HALO)
        for dst, to in ((flat_l, right), (flat_r, left)):
            halo_send(flat_own, dst.at[:, body], (to, lat, dep))
            halo_send(flat_own.at[:, first], dst.at[:, end], (to, above, dep), -1)
            halo_send(flat_own.at[:, last], dst.at[:, top], (to, below, dep), 1)

    flat_sends()
    early_copies = list(h_copies)
    for first, more, n in ((T, 2, 8), (VV, 2, 7), (U, 1, 6)):
        pair = pl.ds(first, more)
        for i in range(first, first + more):
            if i != V:
                wait_load(i)
        halo_send(
            raw.at[pair, pl.ds(HALO, n)], raw.at[pair, pl.ds(HALO + OWN, n)], (lon, above, dep),
            -1,
        )
        halo_send(
            raw.at[pair, pl.ds(HALO + OWN - n, n)], raw.at[pair, pl.ds(HALO - n, n)],
            (lon, below, dep), 1,
        )

    def pack_block(n):
        stores = []
        own = {}
        for r in range(4):
            for i in range(5):
                y = HALO + 4 * n + r
                own[i, r] = pack([raw[i, y, pl.ds(8 * g, 8), :] for g in range(4)])
                stores.append((strips_own, (i, 4 * n + r), own[i, r]))
        for r in range(5):
            tiles = [own[i, r] for i in range(4)] if r < 4 else [own[U, q] for q in range(4)]
            to_right, to_left = pack_four(tiles)
            stores.append((strips_send, (0, 5 * n + r), to_right))
            stores.append((strips_send, (1, 5 * n + r), to_left))
        return stores

    by_rows(0, OWN // 4, 1, pack_block)

    def strip_sends(put, src_r, src_l, dst_l, dst_r, edge):
        body = src_r.shape[-3] if len(src_r.shape) == 3 else src_r.shape[-2]
        sl = (slice(None),) * (0 if len(src_r.shape) == 3 else 1)
        here, first, last = pl.ds(edge, body), pl.ds(0, edge), pl.ds(body - edge, edge)
        after = pl.ds(body + edge, edge)
        put(src_r, dst_l.at[sl + (here,)], (right, lat, dep))
        put(src_l, dst_r.at[sl + (here,)], (left, lat, dep))
        put(src_r.at[sl + (first,)], dst_l.at[sl + (after,)], (right, above, dep), -1)
        put(src_l.at[sl + (first,)], dst_r.at[sl + (after,)], (left, above, dep), -1)
        put(src_r.at[sl + (last,)], dst_l.at[sl + (first,)], (right, below, dep), 1)
        put(src_l.at[sl + (last,)], dst_r.at[sl + (first,)], (left, below, dep), 1)

    strips_from = len(h_copies)
    strip_sends(halo_send, strips_send.at[0], strips_send.at[1], strips_l, strips_r, 10)
    early_copies += h_copies[strips_from:strips_from + 2]
    late_copies = h_copies[len(early_copies) - 2:strips_from] + h_copies[strips_from + 2:]

    finish(a_copies)
    a_dst[0, 0] = a_src[0]
    sums = []
    for slab in range(3):
        total = a_dst[slab, 0]
        for k in range(1, 8):
            total = total + a_dst[slab, k]
        sums.append(total)
    b_src[0] = sums[0]
    b_src[1] = jnp.where(lane % 32 >= 16, sums[1], sums[2])
    b_copies = [
        send(b_src, b_dst.at[k], b_ss.at[k], b_rs.at[k], peer) for k, peer in second_stage
    ]

    def prepare_row(y):
        deep = row(flat, 0, y)
        stores = []
        for g in range(4):
            at = pl.ds(8 * g, 8)
            inside = depth_main[g] < deep
            stores += [
                (mask, (y, at), jnp.where(inside, 1.0 / 12.0, 0.0)),
                (tr, (0, y, at), jnp.where(inside, raw[T, y, at, :], 0.0)),
                (uu, (y, at), jnp.where(inside, 3.0 * raw[UU, y, at, :], 0.0)),
            ]
        return stores

    by_rows(HALO, HALO + OWN, 4, prepare_row)

    finish(early_copies)
    has_above = jnp.where(lat > 0, 1.0, 0.0)
    has_below = jnp.where(lat < NLAT - 1, 1.0, 0.0)
    flat[0, top] = flat[0, top] * has_above
    flat[0, end] = flat[0, end] * has_below
    for y in range(0, ROWS, 8):
        at = pl.ds(y, 8)
        turning = flat[2, at]
        real, imag = jnp.ones((8, 128), F32), jnp.zeros((8, 128), F32)
        for k in range(9):
            coef[2 * k, at] = real
            coef[2 * k + 1, at] = imag
            real, imag = real - turning * imag, imag + turning * real
    for i in range(2):
        for y in range(0, ROWS, 8):
            at = pl.ds(y, 8)
            own = pack([flat[i, at, :]] * 4)
            flat_s[i, at, :] = merge(own, flat_l[i, at, :], flat_r[i, at, :])
    flat_s[0, top] = flat_s[0, top] * has_above
    flat_s[0, end] = flat_s[0, end] * has_below

    def strip_block(n, own):
        stores = []
        for r in range(4):
            y = 4 * n + r
            inside = depth_strip < row(flat_s, 0, y)
            stores.append((s_mask, y, jnp.where(inside, 1.0 / 12.0, 0.0)))
            for i in range(5):
                at, slot = (5 * n + r, i) if i < 4 else (5 * n + 4, r)
                tile = merge(own(i, r), strips_l[at], strips_r[at], slot, slot)
                if i == T:
                    stores.append((s_tr, (0, y), jnp.where(inside, tile, 0.0)))
                    continue
                if i == UU:
                    tile = jnp.where(inside, 3.0 * tile, 0.0)
                stores.append((s_raw, (i, y), tile))
        return stores

    by_rows(
        2, 10, 1, lambda n: strip_block(n, lambda i, r: strips_own[i, 4 * n + r - HALO])
    )
    def slope(kind, low, high, main, strip, main_out, strip_out, fold):
        count = high - low
        got = jnp.dot(
            split(strip(pl.ds(low, count)).reshape(8 * count, 128)),
            strip_mat[kind], preferred_element_type=F32,
        )
        strip_out[pl.ds(low, count)] = got[:, :128].reshape(count, 8, 128)
        edges = [
            got[:, 128 * g + 128:128 * g + 256].reshape(count, 8, 128) for g in range(4)
        ]
        if not fold:
            for g in range(4):
                corr[g, pl.ds(low, count)] = edges[g]
        parts = 4 if count > 8 else 1
        part = count // parts
        for n in range(parts):
            at = pl.ds(low + part * n, part)
            out = jnp.dot(
                split(main(at).reshape(32 * part, 128)), main_mat[kind],
                preferred_element_type=F32,
            ).reshape(part, 32, 128)
            if fold:
                mine = [e[part * n:part * n + part] for e in edges]
                out = out + jnp.concatenate(mine, axis=1)
            main_out[at] = out

    def fixed_slopes(low, high):
        slope(1, low, high, lambda at: uu[at], lambda at: s_raw[UU, at], xu, s_xu, True)
        slope(
            1, low, high, lambda at: 36.0 * mask[at] * raw[VV, at],
            lambda at: 36.0 * s_mask[at] * s_raw[VV, at], xv, s_xv, True,
        )
        slope(
            1, low, high, lambda at: mask[at] * flat[1, at][:, None, :],
            lambda at: s_mask[at] * flat_s[1, at][:, None, :], xb, s_xb, True,
        )

    fixed_slopes(HALO, HALO + OWN)

    finish(b_copies)
    ups = []
    for i in range(2):
        total = b_src[i]
        for k in range(1, RING_Z):
            total = total + b_dst[k, i]
        ups.append(total * thickness * 4.5)

    def gradient(y, up, offset):
        moved = pltpu.roll(up, lax.rem(256 + offset - y, 128), 1)
        spreads = [jnp.broadcast_to(moved[:, 32 * g:32 * g + 1], (8, 128)) for g in range(4)]
        basin = row(flat, 1, y)
        stores = []
        for g in range(4):
            at = pl.ds(8 * g, 8)
            value = mask[y, at, :] * (36.0 * raw[VV, y, at, :] + basin * spreads[g])
            stores.append((vv, (y, at), value))
            stores.append((xv, (y, at), xv[y, at, :] + spreads[g] * xb[y, at, :]))
        joined = spreads[0]
        for g in range(1, 4):
            joined = jnp.where(lane // 32 == g, spreads[g], joined)
        value = s_mask[y] * (36.0 * s_raw[VV, y] + row(flat_s, 1, y) * joined)
        stores.append((s_raw, (VV, y), value))
        stores.append((s_xv, y, s_xv[y] + joined * s_xb[y]))
        return stores

    by_rows(HALO, HALO + OWN, 4, lambda y: gradient(y, ups[0], HALO))
    def column(k, low, high, last, get, emit):
        flux, held, vs = {}, {}, {}

        def reach(y):
            held[y] = get("t", y)
            flux[y] = get("V", y) * held[y]

        def turn(y):
            if k == 0:
                vs[y] = get("v", y)
            else:
                vs[y] = row(coef, 2 * k, y) * get("v", y) + row(coef, 2 * k + 1, y) * get("u", y)

        for y in range(low - 2, low + 2):
            reach(y)
        for y in (low - 1, low):
            turn(y)
        for y in range(low, high):
            reach(y + 2)
            turn(y + 1)
            z_x = get("zx", y)
            if k == 0:
                z_x = z_x + get("xu", y)
            else:
                z_x = z_x + (
                    row(coef, 2 * k, y) * get("xu", y) - row(coef, 2 * k + 1, y) * get("xv", y)
                )
            z_y = 8.0 * (flux[y + 1] - flux[y - 1]) + (vs[y + 1] - vs[y - 1])
            z_y = z_y - (flux[y + 2] - flux[y - 2])
            scale = (1.0 / 12.0) if last else get("m", y)
            emit(y, held[y] + scale * (z_x + z_y))

    def step(k, ranges, last):
        now, new = k % 2, 1 - k % 2
        for low, high in ranges:
            slope(
                0, low, high, lambda at: raw[U, at] * tr[now, at],
                lambda at: s_raw[U, at] * s_tr[now, at], zx, corr.at[4], False,
            )

        def strip_get(what, y):
            return {
                "t": lambda: s_tr[now, y], "u": lambda: s_raw[UU, y], "v": lambda: s_raw[VV, y],
                "m": lambda: s_mask[y], "V": lambda: s_raw[V, y],
                "zx": lambda: corr[4, y], "xu": lambda: s_xu[y], "xv": lambda: s_xv[y],
            }[what]()

        def strip_emit(y, value):
            s_tr[new, y] = value

        if not last:
            for low, high in ranges:
                column(k, low, high, False, strip_get, strip_emit)

        def group(g, c):
            at = pl.ds(pl.multiple_of(8 * g, 8), 8)

            def get(what, y):
                return {
                    "t": lambda: tr[now, y, at, :], "u": lambda: uu[y, at, :],
                    "v": lambda: vv[y, at, :], "m": lambda: mask[y, at, :],
                    "V": lambda: raw[V, y, at, :],
                    "zx": lambda: zx[y, at, :] + corr[g, y],
                    "xu": lambda: xu[y, at, :], "xv": lambda: xv[y, at, :],
                }[what]()

            def emit(y, value):
                tr[new, y, at, :] = value

            for low, high in ranges:
                column(k, low, high, last, get, emit)
            return c

        lax.fori_loop(0, 4, group, 0)

    def inner_rows(k, last):
        for n in range(1, 5):
            step(k + n - 1, ((HALO + 2 * n, HALO + OWN - 2 * n),), last and n == 4)

    def outer_rows(k, last):
        for n in range(1, 5):
            low, high = 2 * n, ROWS - 2 * n
            step(k + n - 1, ((low, low + HALO), (high - HALO, high)), last and n == 4)

    inner_rows(0, False)
    finish(late_copies)
    by_rows(0, HALO, 4, prepare_row)
    by_rows(HALO + OWN, ROWS, 4, prepare_row)
    for outer in (0, ROWS - 2):
        raw[U, pl.ds(outer, 2)] = jnp.zeros((2, 32, 128), F32)
    for outer in (0, ROWS - 1):
        raw[pl.ds(2, 2), outer] = jnp.zeros((2, 32, 128), F32)

    def strip_outer(n):
        return strip_block(
            n, lambda i, r: pack([raw[i, 4 * n + r, pl.ds(8 * g, 8), :] for g in range(4)])
        )

    by_rows(0, 2, 1, strip_outer)
    by_rows(10, 12, 1, strip_outer)

    fixed_slopes(2, HALO)
    fixed_slopes(HALO + OWN, ROWS - 2)
    by_rows(0, HALO, 4, lambda y: gradient(y, ups[1], HALO - OWN))
    by_rows(HALO + OWN, ROWS, 4, lambda y: gradient(y, ups[1], HALO + OWN))
    outer_rows(0, False)

    m_copies = []

    def mid_send(src, dst, peer, toward=0):
        n = len(m_copies)
        m_copies.append(send(src, dst, m_ss.at[n], m_rs.at[n], peer, toward))

    y_src[0] = tr[0, low]
    y_src[1] = tr[0, high]
    mid_send(y_src.at[0], y_dst.at[1], (lon, above, dep), -1)
    mid_send(y_src.at[1], y_dst.at[0], (lon, below, dep), 1)

    def pack_tracer(n):
        own = [
            pack([tr[0, HALO + 4 * n + r, pl.ds(8 * g, 8), :] for g in range(4)])
            for r in range(4)
        ]
        both = pack_four(own)
        return [(o_src, 4 * n + r, own[r]) for r in range(4)] + [
            (o_send, (i, n), both[i]) for i in range(2)
        ]

    by_rows(0, OWN // 4, 2, pack_tracer)
    strip_sends(mid_send, o_send.at[0], o_send.at[1], l_dst, r_dst, 2)

    def turned(y):
        stores = []
        real, imag = row(coef, 16, y) * (1.0 / 3.0), row(coef, 17, y) * (1.0 / 3.0)
        for g in range(4):
            at = pl.ds(8 * g, 8)
            u_0, v_0 = uu[y, at, :], vv[y, at, :]
            stores.append((res, (0, y - HALO, at), real * u_0 - imag * v_0))
            stores.append((res, (1, y - HALO, at), real * v_0 + imag * u_0))
        return stores

    by_rows(HALO, HALO + OWN, 4, turned)

    def store_out(n, held, out):
        def store(z, c):
            pltpu.make_async_copy(held.at[:, z], out.at[z], out_sem.at[n]).start()
            return c
        lax.fori_loop(0, OWN, store, 0)

    store_out(0, res.at[0], out_u)
    store_out(1, res.at[1], out_v)

    finish(m_copies[2:4])

    def own_block(n):
        return [
            (s_tr, (0, HALO + 4 * n + r), merge(o_src[4 * n + r], l_dst[2 + n], r_dst[2 + n], r, r))
            for r in range(4)
        ]

    by_rows(0, OWN // 4, 2, own_block)
    inner_rows(4, True)
    finish(m_copies[:2] + m_copies[4:])

    def halo_block(n):
        stores = []
        for r in range(4):
            for side, at, block, valid in (
                (0, 4 * n + r, n, has_above),
                (1, HALO + OWN + 4 * n + r, 10 + n, has_below),
            ):
                tiles = [y_dst[side, 4 * n + r, pl.ds(8 * g, 8), :] * valid for g in range(4)]
                stores += [(tr, (0, at, pl.ds(8 * g, 8)), tiles[g]) for g in range(4)]
                strip = merge(pack(tiles), l_dst[block] * valid, r_dst[block] * valid, r, r)
                stores.append((s_tr, (0, at), strip))
        return stores

    by_rows(0, 2, 1, halo_block)
    outer_rows(4, True)

    result = tr.at[0, pl.ds(HALO, OWN)]
    store_out(2, result, out_t)
    for n, (held, out) in enumerate(((res.at[0], out_u), (res.at[1], out_v), (result, out_t))):
        pltpu.make_async_copy(held, out, out_sem.at[n]).wait()


def per_device(*args):
    args = args[:7] + (args[7].T, args[8].T) + args[9:]
    block = jax.ShapeDtypeStruct((32, 32, 128), F32)
    main = pltpu.VMEM((ROWS, 32, 128), F32)
    strip = pltpu.VMEM((ROWS, 8, 128), F32)
    dma = pltpu.SemaphoreType.DMA
    return pl.pallas_call(
        kernel,
        out_shape=(block,) * 3,
        in_specs=[pl.BlockSpec(memory_space=pltpu.HBM)] * 11,
        out_specs=(pl.BlockSpec(memory_space=pltpu.HBM),) * 3,
        scratch_shapes=[
            pltpu.VMEM((5, ROWS, 32, 128), F32),
            pltpu.VMEM((2, ROWS, 32, 128), F32),
            main, main, main,
            pltpu.VMEM((5, OWN, 8, 128), F32),
            pltpu.VMEM((2, 40, 8, 128), F32),
            pltpu.VMEM((60, 8, 128), F32),
            pltpu.VMEM((60, 8, 128), F32),
            pltpu.VMEM((5, ROWS, 8, 128), F32),
            strip,
            pltpu.VMEM((2, ROWS, 8, 128), F32),
            main,
            pltpu.VMEM((5, ROWS, 8, 128), F32),
            main, main, main, strip, strip, strip,
            pltpu.VMEM((2, 256, 128), BF16),
            pltpu.VMEM((2, 256, 640), BF16),
            pltpu.VMEM((3, ROWS, 128), F32),
            pltpu.VMEM((18, ROWS, 128), F32),
            pltpu.VMEM((2, OWN, 128), F32),
            pltpu.VMEM((2, ROWS, 128), F32),
            pltpu.VMEM((2, ROWS, 128), F32),
            pltpu.VMEM((2, ROWS, 128), F32),
            pltpu.VMEM((2, OWN, 128), jnp.int32),
            pltpu.VMEM((2, 32, 64), F32),
            pltpu.SMEM((32,), F32),
            pltpu.SMEM((32,), F32),
            pltpu.VMEM((2, 8, 128), F32),
            pltpu.VMEM((3, 8, 8, 128), F32),
            pltpu.VMEM((2, 8, 128), F32),
            pltpu.VMEM((8, 2, 8, 128), F32),
            pltpu.VMEM((2, HALO, 32, 128), F32),
            pltpu.VMEM((2, HALO, 32, 128), F32),
            pltpu.VMEM((OWN, 8, 128), F32),
            pltpu.VMEM((2, 8, 8, 128), F32),
            pltpu.VMEM((12, 8, 128), F32),
            pltpu.VMEM((12, 8, 128), F32),
            pltpu.VMEM((2, OWN, 32, 128), F32),
            dma((5,)), dma((6,)), dma((24,)), dma((24,)), dma((8,)), dma((8,)),
            dma((20,)), dma((20,)), dma((8,)), dma((8,)), dma((3,)),
        ],
        compiler_params=pltpu.CompilerParams(
            collective_id=0, has_side_effects=True, vmem_limit_bytes=60 * 1024 * 1024
        ),
        name="adjoint",
    )(*args)


def solution(mesh):
    block, level = P("dep", "lat", "lon"), P(None, "lat")
    in_specs = (block,) * 5 + (P("lat"), P("dep"), level, level) + (P("lat", "lon"),) * 2
    return jax.shard_map(
        per_device, mesh=mesh, in_specs=in_specs, out_specs=(block,) * 3, check_vma=False
    )
```

```python
import jax
import jax.numpy as jnp
from jax import lax
from jax.experimental import pallas as pl
from jax.experimental.pallas import tpu as pltpu
from jax.sharding import PartitionSpec as P

MESH = pl.DeviceIdType.MESH
F32 = jnp.float32
BF16 = jnp.bfloat16
HALO = 8
OWN = 32
ROWS = OWN + 2 * HALO
NLON, NLAT, NDEP = 32, 4, 2
RING_Y, RING_Z = 4, 8
T, V, VV, UU, U = range(5)


def lanes():
    return lax.broadcasted_iota(jnp.int32, (8, 128), 1)


def sublanes():
    return lax.broadcasted_iota(jnp.int32, (8, 128), 0)


def lroll(x, shift):
    shift = shift % 128
    return x if shift == 0 else pltpu.roll(x, shift, 1)


def sroll(x, shift):
    return pltpu.roll(x, shift % 8, 0)


def pack(tiles):
    at = (lanes() + 8) // 32 % 4
    joined = tiles[0]
    for g in range(1, 4):
        joined = jnp.where(at == g, lroll(tiles[g], 32 * g), joined)
    return jnp.where(lanes() % 32 < 16, lroll(joined, 8), lroll(joined, 24))


def merge(own, left, right, slot=2, other=1):
    place = lanes() % 32
    return jnp.where(
        place < 8,
        lroll(left, -8 * slot),
        jnp.where(place >= 24, lroll(right, 24 - 8 * other), own),
    )


def pack_four(strips):
    at = lanes() // 8 % 4
    both = []
    for base in (16, 8):
        joined = lroll(strips[0], -base)
        for j in range(1, 4):
            joined = jnp.where(at == j, lroll(strips[j], 8 * j - base), joined)
        both.append(joined)
    return both


def slope_matrix(kind, group):
    i = lax.broadcasted_iota(jnp.int32, (128, 128), 0)
    j = lax.broadcasted_iota(jnp.int32, (128, 128), 1)
    if group is not None:
        place = i % 32
        halo = jnp.logical_or(place < 8, place >= 24)
        here = jnp.logical_and(halo, i // 32 == group)
        i = jnp.where(here, jnp.where(place < 8, place - 8, place + 104), 1000)
    apart = i - j
    near, far = (8.0, 1.0) if kind == 0 else (1.0, 0.0)
    out = jnp.where(apart == 1, near, jnp.where(apart == -1, -near, 0.0))
    return out + jnp.where(apart == 2, -far, jnp.where(apart == -2, far, 0.0))


def split(x):
    high = x.astype(BF16)
    return jnp.concatenate([high, (x - high.astype(F32)).astype(BF16)], axis=1)


def suffix_tile(x):
    lane, sub = lanes(), sublanes()
    for k in (1, 2, 4):
        x = x + jnp.where(sub < 8 - k, sroll(x, -k), 0.0)
    group = jnp.broadcast_to(x[0:1, :], (8, 128))
    out, total = x, group
    for j in (1, 2, 3):
        moved = lroll(group, -32 * j)
        out = out + jnp.where(lane < 128 - 32 * j, moved, 0.0)
        total = total + moved
    return out, total


def prefix_tile(x):
    lane, sub = lanes(), sublanes()
    for k in (1, 2, 4):
        x = x + jnp.where(sub >= k, sroll(x, k), 0.0)
    group = jnp.broadcast_to(x[7:8, :], (8, 128))
    out, total = x, group
    for j in (1, 2, 3):
        moved = lroll(group, 32 * j)
        out = out + jnp.where(lane >= 32 * j, moved, 0.0)
        total = total + moved
    return out, total


def by_rows(low, high, block, fn):
    def body(n, c):
        stores = []
        for r in range(block):
            stores += fn(low + block * n + r)
        for ref, index, value in stores:
            ref[index] = value
        return c

    lax.fori_loop(0, (high - low) // block, body, 0)


def reduce_lanes(make):
    lane = lanes()

    def tree(level, start):
        if level < 0:
            return make(start)
        step = 1 << level
        a = tree(level - 1, start)
        b = tree(level - 1, start + step)
        even = (lane & step) == 0
        return jnp.where(even, a, b) + lroll(jnp.where(even, b, a), -step)

    return tree(6, 0)


def kernel(
    adj_u, adj_v, adj_t, zonal, merid, cor, thick, weight_t, target_t, atl, bottom,
    out_u, out_v, out_t,
    raw, tr, uu, vv, mask, strips_own, strips_send, strips_l, strips_r, s_raw, s_mask, s_tr,
    zx, corr, xu, xv, xb, s_xu, s_xv, s_xb, main_mat, strip_mat,
    flat, coef, flat_own, flat_l, flat_r, flat_s, ints, wt, cor_s, thick_s,
    a_src, a_dst, b_src, b_dst, y_src, y_dst, o_src, o_send, l_dst, r_dst,
    load_sem, small_sem, a_ss, a_rs, b_ss, b_rs, h_ss, h_rs, m_ss, m_rs,
):
    lon, lat, dep = lax.axis_index("lon"), lax.axis_index("lat"), lax.axis_index("dep")
    ring_y, ring_z = lon % RING_Y, lon // RING_Y

    sources = (adj_t, merid, adj_v, adj_u, zonal)
    for i in (V, T, VV, UU, U):
        def load(z, c, i=i):
            pltpu.make_async_copy(
                sources[i].at[z], raw.at[i, pl.ds(HALO, OWN), z], load_sem.at[i]
            ).start()
            return c
        if i == V:
            smalls = [
                pltpu.make_async_copy(bottom, ints.at[0], small_sem.at[0]),
                pltpu.make_async_copy(atl, ints.at[1], small_sem.at[1]),
                pltpu.make_async_copy(weight_t, wt.at[0], small_sem.at[2]),
                pltpu.make_async_copy(target_t, wt.at[1], small_sem.at[3]),
                pltpu.make_async_copy(cor, cor_s, small_sem.at[4]),
                pltpu.make_async_copy(thick, thick_s, small_sem.at[5]),
            ]
            for copy in smalls:
                copy.start()
        lax.fori_loop(0, OWN, load, 0)

    def wait_load(i):
        pltpu.make_async_copy(
            sources[i], raw.at[i, pl.ds(HALO, OWN)], load_sem.at[i]
        ).wait()

    def wrap(i, n):
        return lax.rem(i + n, n)

    def ring_y_peer(k):
        return ring_z * RING_Y + lax.rem(ring_y + k, RING_Y)

    right, left = wrap(lon + 1, NLON), wrap(lon - 1, NLON)
    above, below = wrap(lat - 1, NLAT), wrap(lat + 1, NLAT)
    first_stage = []
    for slab, to_lat in ((0, lat), (1, below), (2, above)):
        for k in range(RING_Y):
            for d in range(NDEP):
                if slab == 0 and k == 0 and d == 0:
                    continue
                to_dep = dep if d == 0 else 1 - dep
                first_stage.append((slab, 2 * k + d, d, (ring_y_peer(k), to_lat, to_dep)))
    second_stage = [
        (k, (lax.rem(lon + RING_Y * k, NLON), lat, dep)) for k in range(1, RING_Z)
    ]
    around = [
        (right, lat, dep), (left, lat, dep),
        (right, above, dep), (left, above, dep), (right, below, dep), (left, below, dep),
    ]
    barrier = pltpu.get_barrier_semaphore()
    greeted = [p[3] for p in first_stage] + [p[1] for p in second_stage] + around
    for peer in greeted:
        pl.semaphore_signal(barrier, inc=1, device_id=peer, device_id_type=MESH)

    lane, sub = lanes(), sublanes()
    for copy in smalls:
        copy.wait()
    for y in range(0, OWN, 8):
        flat[0, pl.ds(HALO + y, 8)] = ints[0, pl.ds(y, 8)].astype(F32)
        flat[1, pl.ds(HALO + y, 8)] = ints[1, pl.ds(y, 8)].astype(F32)
        turning = jnp.zeros((8, 128), F32)
        for r in range(8):
            turning = jnp.where(sub == r, cor_s[y + r], turning)
        flat[2, pl.ds(HALO + y, 8)] = turning
    thickness = jnp.zeros((8, 128), F32)
    for z in range(OWN):
        here = jnp.logical_and(sub == z % 8, lane // 32 == z // 8)
        thickness = jnp.where(here, thick_s[z], thickness)

    for kind in range(2):
        for n in range(5):
            mat = slope_matrix(kind, None if n == 0 else n - 1).astype(BF16)
            for half in range(2):
                strip_mat[kind, pl.ds(128 * half, 128), pl.ds(128 * n, 128)] = mat
                if n == 0:
                    main_mat[kind, pl.ds(128 * half, 128), :] = mat

    depth_main = [(dep * OWN + 8 * g + sub).astype(F32) for g in range(4)]
    depth_strip = (dep * OWN + 8 * (lane // 32) + sub).astype(F32)

    def row(ref, i, y):
        return jnp.broadcast_to(ref[i, pl.ds(y, 1), :], (8, 128))

    wait_load(V)

    def basin_flow(i):
        g, y = i // OWN, HALO + i % OWN
        inside = depth_main[g] < row(flat, 0, y)
        return jnp.where(inside, raw[V, y, pl.ds(8 * g, 8), :], 0.0) * row(flat, 1, y)

    level_sum = reduce_lanes(basin_flow) * thickness

    def packed(i):
        filled = jnp.concatenate([wt[i], jnp.zeros((32, 64), F32)], axis=1)
        filled = jnp.concatenate([filled, jnp.zeros((96, 128), F32)], axis=0)
        turned = filled.T
        halves = []
        for half in range(2):
            tile = turned[32 * half:32 * half + 8]
            for g in range(1, 4):
                start = 32 * half + 8 * g
                tile = jnp.where(lane // 32 == g, lroll(turned[start:start + 8], 32 * g), tile)
            halves.append(tile)
        lower = dep == 1
        return jnp.where(lower, halves[1], halves[0]), jnp.where(lower, halves[0], halves[1])

    w_own, w_other = packed(0)
    g_own, g_other = packed(1)
    deeper, whole = suffix_tile(level_sum)
    is_low = jnp.where(dep == 1, 1.0, 0.0)
    mis_own = w_own * (deeper * (1.0 / 512.0) - g_own * (1.0 / 64.0))
    mis_other = w_other * (whole * is_low * (1.0 / 512.0) - g_other * (1.0 / 64.0))
    up_own, tot_own = prefix_tile(mis_own)
    up_other, tot_other = prefix_tile(mis_other)
    a_src[0] = up_own + is_low * tot_other
    a_src[1] = up_other + (1.0 - is_low) * tot_own

    def clear(rows, tiles, few, side, slab):
        raw[:, rows] = jnp.zeros((5, HALO, 32, 128), F32)
        flat[:, rows] = jnp.zeros((3, HALO, 128), F32)
        a_dst[slab] = jnp.zeros((8, 8, 128), F32)
        y_dst[side] = jnp.zeros((HALO, 32, 128), F32)
        for ref in (strips_l, strips_r):
            ref[tiles] = jnp.zeros((10, 8, 128), F32)
        for ref in (flat_l, flat_r):
            ref[:, rows] = jnp.zeros((2, HALO, 128), F32)
        for ref in (l_dst, r_dst):
            ref[few] = jnp.zeros((2, 8, 128), F32)

    @pl.when(lat == 0)
    def _():
        clear(pl.ds(0, HALO), pl.ds(0, 10), pl.ds(0, 2), 0, 1)

    @pl.when(lat == NLAT - 1)
    def _():
        clear(pl.ds(HALO + OWN, HALO), pl.ds(50, 10), pl.ds(10, 2), 1, 2)

    pl.semaphore_wait(barrier, len(greeted))

    inner = {-1: lat > 0, 1: lat < NLAT - 1}

    def when(condition, act):
        if condition is None:
            act()
        else:
            pl.when(condition)(act)

    def send(src, dst, ss, rs, peer, toward=0):
        copy = pltpu.make_async_remote_copy(
            src_ref=src, dst_ref=dst, send_sem=ss, recv_sem=rs,
            device_id=peer, device_id_type=MESH,
        )
        when(inner.get(toward), copy.start)
        return copy, toward

    def finish(copies):
        for copy, toward in copies:
            when(inner.get(-toward), copy.wait_recv)
        for copy, toward in copies:
            when(inner.get(toward), copy.wait_send)

    a_copies = [
        send(a_src.at[d], a_dst.at[slab, slot], a_ss.at[8 * slab + slot], a_rs.at[8 * slab + slot], peer, (0, 1, -1)[slab])
        for slab, slot, d, peer in first_stage
    ]

    h_copies = []

    def halo_send(src, dst, peer, toward=0):
        n = len(h_copies)
        h_copies.append(send(src, dst, h_ss.at[n], h_rs.at[n], peer, toward))

    low, high = pl.ds(HALO, HALO), pl.ds(OWN, HALO)
    top, end = pl.ds(0, HALO), pl.ds(HALO + OWN, HALO)
    halo_send(flat.at[:, low], flat.at[:, end], (lon, above, dep), -1)
    halo_send(flat.at[:, high], flat.at[:, top], (lon, below, dep), 1)
    for i in range(2):
        for y in range(0, OWN, 8):
            tile = flat[i, pl.ds(HALO + y, 8), :]
            flat_own[i, pl.ds(y, 8), :] = pack([tile] * 4)

    def flat_sends():
        body, first, last = pl.ds(HALO, OWN), pl.ds(0, HALO), pl.ds(OWN - HALO, HALO)
        for dst, to in ((flat_l, right), (flat_r, left)):
            halo_send(flat_own, dst.at[:, body], (to, lat, dep))
            halo_send(flat_own.at[:, first], dst.at[:, end], (to, above, dep), -1)
            halo_send(flat_own.at[:, last], dst.at[:, top], (to, below, dep), 1)

    flat_sends()
    early_copies = list(h_copies)
    for first, more, n in ((T, 2, 8), (VV, 2, 7), (U, 1, 6)):
        pair = pl.ds(first, more)
        for i in range(first, first + more):
            if i != V:
                wait_load(i)
        halo_send(
            raw.at[pair, pl.ds(HALO, n)], raw.at[pair, pl.ds(HALO + OWN, n)], (lon, above, dep),
            -1,
        )
        halo_send(
            raw.at[pair, pl.ds(HALO + OWN - n, n)], raw.at[pair, pl.ds(HALO - n, n)],
            (lon, below, dep), 1,
        )

    def pack_block(n):
        stores = []
        own = {}
        for r in range(4):
            for i in range(5):
                y = HALO + 4 * n + r
                own[i, r] = pack([raw[i, y, pl.ds(8 * g, 8), :] for g in range(4)])
                stores.append((strips_own, (i, 4 * n + r), own[i, r]))
        for r in range(5):
            tiles = [own[i, r] for i in range(4)] if r < 4 else [own[U, q] for q in range(4)]
            to_right, to_left = pack_four(tiles)
            stores.append((strips_send, (0, 5 * n + r), to_right))
            stores.append((strips_send, (1, 5 * n + r), to_left))
        return stores

    by_rows(0, OWN // 4, 1, pack_block)

    def strip_sends(put, src_r, src_l, dst_l, dst_r, edge):
        body = src_r.shape[-3] if len(src_r.shape) == 3 else src_r.shape[-2]
        sl = (slice(None),) * (0 if len(src_r.shape) == 3 else 1)
        here, first, last = pl.ds(edge, body), pl.ds(0, edge), pl.ds(body - edge, edge)
        after = pl.ds(body + edge, edge)
        put(src_r, dst_l.at[sl + (here,)], (right, lat, dep))
        put(src_l, dst_r.at[sl + (here,)], (left, lat, dep))
        put(src_r.at[sl + (first,)], dst_l.at[sl + (after,)], (right, above, dep), -1)
        put(src_l.at[sl + (first,)], dst_r.at[sl + (after,)], (left, above, dep), -1)
        put(src_r.at[sl + (last,)], dst_l.at[sl + (first,)], (right, below, dep), 1)
        put(src_l.at[sl + (last,)], dst_r.at[sl + (first,)], (left, below, dep), 1)

    strips_from = len(h_copies)
    strip_sends(halo_send, strips_send.at[0], strips_send.at[1], strips_l, strips_r, 10)
    early_copies += h_copies[strips_from:strips_from + 2]
    late_copies = h_copies[len(early_copies) - 2:strips_from] + h_copies[strips_from + 2:]

    finish(a_copies)
    a_dst[0, 0] = a_src[0]
    sums = []
    for slab in range(3):
        total = a_dst[slab, 0]
        for k in range(1, 8):
            total = total + a_dst[slab, k]
        sums.append(total)
    b_src[0] = sums[0]
    b_src[1] = jnp.where(lane % 32 >= 16, sums[1], sums[2])
    b_copies = [
        send(b_src, b_dst.at[k], b_ss.at[k], b_rs.at[k], peer) for k, peer in second_stage
    ]

    def prepare_row(y):
        deep = row(flat, 0, y)
        stores = []
        for g in range(4):
            at = pl.ds(8 * g, 8)
            inside = depth_main[g] < deep
            stores += [
                (mask, (y, at), jnp.where(inside, 1.0 / 12.0, 0.0)),
                (tr, (0, y, at), jnp.where(inside, raw[T, y, at, :], 0.0)),
                (uu, (y, at), jnp.where(inside, 3.0 * raw[UU, y, at, :], 0.0)),
            ]
        return stores

    by_rows(HALO, HALO + OWN, 4, prepare_row)

    finish(early_copies)
    has_above = jnp.where(lat > 0, 1.0, 0.0)
    has_below = jnp.where(lat < NLAT - 1, 1.0, 0.0)
    flat[0, top] = flat[0, top] * has_above
    flat[0, end] = flat[0, end] * has_below
    for y in range(0, ROWS, 8):
        at = pl.ds(y, 8)
        turning = flat[2, at]
        real, imag = jnp.ones((8, 128), F32), jnp.zeros((8, 128), F32)
        for k in range(9):
            coef[2 * k, at] = real
            coef[2 * k + 1, at] = imag
            real, imag = real - turning * imag, imag + turning * real
    for i in range(2):
        for y in range(0, ROWS, 8):
            at = pl.ds(y, 8)
            own = pack([flat[i, at, :]] * 4)
            flat_s[i, at, :] = merge(own, flat_l[i, at, :], flat_r[i, at, :])
    flat_s[0, top] = flat_s[0, top] * has_above
    flat_s[0, end] = flat_s[0, end] * has_below

    def strip_block(n, own):
        stores = []
        for r in range(4):
            y = 4 * n + r
            inside = depth_strip < row(flat_s, 0, y)
            stores.append((s_mask, y, jnp.where(inside, 1.0 / 12.0, 0.0)))
            for i in range(5):
                at, slot = (5 * n + r, i) if i < 4 else (5 * n + 4, r)
                tile = merge(own(i, r), strips_l[at], strips_r[at], slot, slot)
                if i == T:
                    stores.append((s_tr, (0, y), jnp.where(inside, tile, 0.0)))
                    continue
                if i == UU:
                    tile = jnp.where(inside, 3.0 * tile, 0.0)
                stores.append((s_raw, (i, y), tile))
        return stores

    by_rows(
        2, 10, 1, lambda n: strip_block(n, lambda i, r: strips_own[i, 4 * n + r - HALO])
    )
    def slope(kind, low, high, main, strip, main_out, strip_out, fold):
        count = high - low
        got = jnp.dot(
            split(strip(pl.ds(low, count)).reshape(8 * count, 128)),
            strip_mat[kind], preferred_element_type=F32,
        )
        strip_out[pl.ds(low, count)] = got[:, :128].reshape(count, 8, 128)
        edges = [
            got[:, 128 * g + 128:128 * g + 256].reshape(count, 8, 128) for g in range(4)
        ]
        if not fold:
            for g in range(4):
                corr[g, pl.ds(low, count)] = edges[g]
        parts = 4 if count > 8 else 1
        part = count // parts
        for n in range(parts):
            at = pl.ds(low + part * n, part)
            out = jnp.dot(
                split(main(at).reshape(32 * part, 128)), main_mat[kind],
                preferred_element_type=F32,
            ).reshape(part, 32, 128)
            if fold:
                mine = [e[part * n:part * n + part] for e in edges]
                out = out + jnp.concatenate(mine, axis=1)
            main_out[at] = out

    def fixed_slopes(low, high):
        slope(1, low, high, lambda at: uu[at], lambda at: s_raw[UU, at], xu, s_xu, True)
        slope(
            1, low, high, lambda at: 36.0 * mask[at] * raw[VV, at],
            lambda at: 36.0 * s_mask[at] * s_raw[VV, at], xv, s_xv, True,
        )
        slope(
            1, low, high, lambda at: mask[at] * flat[1, at][:, None, :],
            lambda at: s_mask[at] * flat_s[1, at][:, None, :], xb, s_xb, True,
        )

    fixed_slopes(HALO, HALO + OWN)

    finish(b_copies)
    ups = []
    for i in range(2):
        total = b_src[i]
        for k in range(1, RING_Z):
            total = total + b_dst[k, i]
        ups.append(total * thickness * 4.5)

    def gradient(y, up, offset):
        moved = pltpu.roll(up, lax.rem(256 + offset - y, 128), 1)
        spreads = [jnp.broadcast_to(moved[:, 32 * g:32 * g + 1], (8, 128)) for g in range(4)]
        basin = row(flat, 1, y)
        stores = []
        for g in range(4):
            at = pl.ds(8 * g, 8)
            value = mask[y, at, :] * (36.0 * raw[VV, y, at, :] + basin * spreads[g])
            stores.append((vv, (y, at), value))
            stores.append((xv, (y, at), xv[y, at, :] + spreads[g] * xb[y, at, :]))
        joined = spreads[0]
        for g in range(1, 4):
            joined = jnp.where(lane // 32 == g, spreads[g], joined)
        value = s_mask[y] * (36.0 * s_raw[VV, y] + row(flat_s, 1, y) * joined)
        stores.append((s_raw, (VV, y), value))
        stores.append((s_xv, y, s_xv[y] + joined * s_xb[y]))
        return stores

    by_rows(HALO, HALO + OWN, 4, lambda y: gradient(y, ups[0], HALO))
    def column(k, low, high, last, get, emit):
        flux, held, vs = {}, {}, {}

        def reach(y):
            held[y] = get("t", y)
            flux[y] = get("V", y) * held[y]

        def turn(y):
            if k == 0:
                vs[y] = get("v", y)
            else:
                vs[y] = row(coef, 2 * k, y) * get("v", y) + row(coef, 2 * k + 1, y) * get("u", y)

        for y in range(low - 2, low + 2):
            reach(y)
        for y in (low - 1, low):
            turn(y)
        for y in range(low, high):
            reach(y + 2)
            turn(y + 1)
            z_x = get("zx", y)
            if k == 0:
                z_x = z_x + get("xu", y)
            else:
                z_x = z_x + (
                    row(coef, 2 * k, y) * get("xu", y) - row(coef, 2 * k + 1, y) * get("xv", y)
                )
            z_y = 8.0 * (flux[y + 1] - flux[y - 1]) + (vs[y + 1] - vs[y - 1])
            z_y = z_y - (flux[y + 2] - flux[y - 2])
            scale = (1.0 / 12.0) if last else get("m", y)
            emit(y, held[y] + scale * (z_x + z_y))

    def step(k, ranges, last):
        now, new = k % 2, 1 - k % 2
        for low, high in ranges:
            slope(
                0, low, high, lambda at: raw[U, at] * tr[now, at],
                lambda at: s_raw[U, at] * s_tr[now, at], zx, corr.at[4], False,
            )

        def strip_get(what, y):
            return {
                "t": lambda: s_tr[now, y], "u": lambda: s_raw[UU, y], "v": lambda: s_raw[VV, y],
                "m": lambda: s_mask[y], "V": lambda: s_raw[V, y],
                "zx": lambda: corr[4, y], "xu": lambda: s_xu[y], "xv": lambda: s_xv[y],
            }[what]()

        def strip_emit(y, value):
            s_tr[new, y] = value

        if not last:
            for low, high in ranges:
                column(k, low, high, False, strip_get, strip_emit)

        def group(g, c):
            at = pl.ds(pl.multiple_of(8 * g, 8), 8)

            def get(what, y):
                return {
                    "t": lambda: tr[now, y, at, :], "u": lambda: uu[y, at, :],
                    "v": lambda: vv[y, at, :], "m": lambda: mask[y, at, :],
                    "V": lambda: raw[V, y, at, :],
                    "zx": lambda: zx[y, at, :] + corr[g, y],
                    "xu": lambda: xu[y, at, :], "xv": lambda: xv[y, at, :],
                }[what]()

            def emit(y, value):
                if last:
                    out_t[y - HALO, at, :] = value
                else:
                    tr[new, y, at, :] = value

            for low, high in ranges:
                column(k, low, high, last, get, emit)
            return c

        lax.fori_loop(0, 4, group, 0)

    def inner_rows(k, last):
        for n in range(1, 5):
            step(k + n - 1, ((HALO + 2 * n, HALO + OWN - 2 * n),), last and n == 4)

    def outer_rows(k, last):
        for n in range(1, 5):
            low, high = 2 * n, ROWS - 2 * n
            step(k + n - 1, ((low, low + HALO), (high - HALO, high)), last and n == 4)

    inner_rows(0, False)
    finish(late_copies)
    by_rows(0, HALO, 4, prepare_row)
    by_rows(HALO + OWN, ROWS, 4, prepare_row)
    for outer in (0, ROWS - 2):
        raw[U, pl.ds(outer, 2)] = jnp.zeros((2, 32, 128), F32)
    for outer in (0, ROWS - 1):
        raw[pl.ds(2, 2), outer] = jnp.zeros((2, 32, 128), F32)

    def strip_outer(n):
        return strip_block(
            n, lambda i, r: pack([raw[i, 4 * n + r, pl.ds(8 * g, 8), :] for g in range(4)])
        )

    by_rows(0, 2, 1, strip_outer)
    by_rows(10, 12, 1, strip_outer)

    fixed_slopes(2, HALO)
    fixed_slopes(HALO + OWN, ROWS - 2)
    by_rows(0, HALO, 4, lambda y: gradient(y, ups[1], HALO - OWN))
    by_rows(HALO + OWN, ROWS, 4, lambda y: gradient(y, ups[1], HALO + OWN))
    outer_rows(0, False)

    m_copies = []

    def mid_send(src, dst, peer, toward=0):
        n = len(m_copies)
        m_copies.append(send(src, dst, m_ss.at[n], m_rs.at[n], peer, toward))

    y_src[0] = tr[0, low]
    y_src[1] = tr[0, high]
    mid_send(y_src.at[0], y_dst.at[1], (lon, above, dep), -1)
    mid_send(y_src.at[1], y_dst.at[0], (lon, below, dep), 1)

    def pack_tracer(n):
        own = [
            pack([tr[0, HALO + 4 * n + r, pl.ds(8 * g, 8), :] for g in range(4)])
            for r in range(4)
        ]
        both = pack_four(own)
        return [(o_src, 4 * n + r, own[r]) for r in range(4)] + [
            (o_send, (i, n), both[i]) for i in range(2)
        ]

    by_rows(0, OWN // 4, 2, pack_tracer)
    strip_sends(mid_send, o_send.at[0], o_send.at[1], l_dst, r_dst, 2)

    def turned(y):
        stores = []
        real, imag = row(coef, 16, y) * (1.0 / 3.0), row(coef, 17, y) * (1.0 / 3.0)
        for g in range(4):
            at = pl.ds(8 * g, 8)
            u_0, v_0 = uu[y, at, :], vv[y, at, :]
            stores.append((out_u, (y - HALO, at), real * u_0 - imag * v_0))
            stores.append((out_v, (y - HALO, at), real * v_0 + imag * u_0))
        return stores

    by_rows(HALO, HALO + OWN, 4, turned)

    finish(m_copies[2:4])

    def own_block(n):
        return [
            (s_tr, (0, HALO + 4 * n + r), merge(o_src[4 * n + r], l_dst[2 + n], r_dst[2 + n], r, r))
            for r in range(4)
        ]

    by_rows(0, OWN // 4, 2, own_block)
    inner_rows(4, True)
    finish(m_copies[:2] + m_copies[4:])

    def halo_block(n):
        stores = []
        for r in range(4):
            for side, at, block, valid in (
                (0, 4 * n + r, n, has_above),
                (1, HALO + OWN + 4 * n + r, 10 + n, has_below),
            ):
                tiles = [y_dst[side, 4 * n + r, pl.ds(8 * g, 8), :] * valid for g in range(4)]
                stores += [(tr, (0, at, pl.ds(8 * g, 8)), tiles[g]) for g in range(4)]
                strip = merge(pack(tiles), l_dst[block] * valid, r_dst[block] * valid, r, r)
                stores.append((s_tr, (0, at), strip))
        return stores

    by_rows(0, 2, 1, halo_block)
    outer_rows(4, True)


def store(*refs):
    held, outs, sem = refs[:3], refs[3:6], refs[6]
    for n in range(3):
        def level(z, c, n=n):
            pltpu.make_async_copy(held[n].at[:, z], outs[n].at[z], sem.at[n]).start()
            return c
        lax.fori_loop(0, OWN, level, 0)
    for n in range(3):
        pltpu.make_async_copy(held[n], outs[n], sem.at[n]).wait()


def per_device(*args):
    args = args[:7] + (args[7].T, args[8].T) + args[9:]
    held = pltpu.VMEM((32, 32, 128), F32)
    main = pltpu.VMEM((ROWS, 32, 128), F32)
    strip = pltpu.VMEM((ROWS, 8, 128), F32)
    dma = pltpu.SemaphoreType.DMA
    results = pl.pallas_call(
        kernel,
        out_shape=(held,) * 3,
        in_specs=[pl.BlockSpec(memory_space=pltpu.HBM)] * 11,
        out_specs=(pl.BlockSpec(memory_space=pltpu.VMEM),) * 3,
        scratch_shapes=[
            pltpu.VMEM((5, ROWS, 32, 128), F32),
            pltpu.VMEM((2, ROWS, 32, 128), F32),
            main, main, main,
            pltpu.VMEM((5, OWN, 8, 128), F32),
            pltpu.VMEM((2, 40, 8, 128), F32),
            pltpu.VMEM((60, 8, 128), F32),
            pltpu.VMEM((60, 8, 128), F32),
            pltpu.VMEM((5, ROWS, 8, 128), F32),
            strip,
            pltpu.VMEM((2, ROWS, 8, 128), F32),
            main,
            pltpu.VMEM((5, ROWS, 8, 128), F32),
            main, main, main, strip, strip, strip,
            pltpu.VMEM((2, 256, 128), BF16),
            pltpu.VMEM((2, 256, 640), BF16),
            pltpu.VMEM((3, ROWS, 128), F32),
            pltpu.VMEM((18, ROWS, 128), F32),
            pltpu.VMEM((2, OWN, 128), F32),
            pltpu.VMEM((2, ROWS, 128), F32),
            pltpu.VMEM((2, ROWS, 128), F32),
            pltpu.VMEM((2, ROWS, 128), F32),
            pltpu.VMEM((2, OWN, 128), jnp.int32),
            pltpu.VMEM((2, 32, 64), F32),
            pltpu.SMEM((32,), F32),
            pltpu.SMEM((32,), F32),
            pltpu.VMEM((2, 8, 128), F32),
            pltpu.VMEM((3, 8, 8, 128), F32),
            pltpu.VMEM((2, 8, 128), F32),
            pltpu.VMEM((8, 2, 8, 128), F32),
            pltpu.VMEM((2, HALO, 32, 128), F32),
            pltpu.VMEM((2, HALO, 32, 128), F32),
            pltpu.VMEM((OWN, 8, 128), F32),
            pltpu.VMEM((2, 8, 8, 128), F32),
            pltpu.VMEM((12, 8, 128), F32),
            pltpu.VMEM((12, 8, 128), F32),
            dma((5,)), dma((6,)), dma((24,)), dma((24,)), dma((8,)), dma((8,)),
            dma((20,)), dma((20,)), dma((8,)), dma((8,)),
        ],
        compiler_params=pltpu.CompilerParams(
            collective_id=0, has_side_effects=True, vmem_limit_bytes=60 * 1024 * 1024
        ),
        name="adjoint",
    )(*args)
    return pl.pallas_call(
        store,
        out_shape=(jax.ShapeDtypeStruct((32, 32, 128), F32),) * 3,
        in_specs=[pl.BlockSpec(memory_space=pltpu.VMEM)] * 3,
        out_specs=(pl.BlockSpec(memory_space=pltpu.HBM),) * 3,
        scratch_shapes=[dma((3,))],
        compiler_params=pltpu.CompilerParams(vmem_limit_bytes=4 * 1024 * 1024),
        name="store",
    )(*results)


def solution(mesh):
    block, level = P("dep", "lat", "lon"), P(None, "lat")
    in_specs = (block,) * 5 + (P("lat"), P("dep"), level, level) + (P("lat", "lon"),) * 2
    return jax.shard_map(
        per_device, mesh=mesh, in_specs=in_specs, out_specs=(block,) * 3, check_vma=False
    )
```

```python
import jax
import jax.numpy as jnp
from jax import lax
from jax.experimental import pallas as pl
from jax.experimental.pallas import tpu as pltpu
from jax.sharding import PartitionSpec as P

MESH = pl.DeviceIdType.MESH
F32 = jnp.float32
BF16 = jnp.bfloat16
HALO = 8
OWN = 32
ROWS = OWN + 2 * HALO
NLON, NLAT, NDEP = 32, 4, 2
RING_Y, RING_Z = 4, 8
T, V, VV, UU, U = range(5)


def lanes():
    return lax.broadcasted_iota(jnp.int32, (8, 128), 1)


def sublanes():
    return lax.broadcasted_iota(jnp.int32, (8, 128), 0)


def lroll(x, shift):
    shift = shift % 128
    return x if shift == 0 else pltpu.roll(x, shift, 1)


def sroll(x, shift):
    return pltpu.roll(x, shift % 8, 0)


def pack(tiles):
    at = (lanes() + 8) // 32 % 4
    joined = tiles[0]
    for g in range(1, 4):
        joined = jnp.where(at == g, lroll(tiles[g], 32 * g), joined)
    return jnp.where(lanes() % 32 < 16, lroll(joined, 8), lroll(joined, 24))


def merge(own, left, right, slot=2, other=1):
    place = lanes() % 32
    return jnp.where(
        place < 8,
        lroll(left, -8 * slot),
        jnp.where(place >= 24, lroll(right, 24 - 8 * other), own),
    )


def pack_four(strips):
    at = lanes() // 8 % 4
    both = []
    for base in (16, 8):
        joined = lroll(strips[0], -base)
        for j in range(1, 4):
            joined = jnp.where(at == j, lroll(strips[j], 8 * j - base), joined)
        both.append(joined)
    return both


def slope_matrix(kind, group):
    i = lax.broadcasted_iota(jnp.int32, (128, 128), 0)
    j = lax.broadcasted_iota(jnp.int32, (128, 128), 1)
    if group is not None:
        place = i % 32
        halo = jnp.logical_or(place < 8, place >= 24)
        here = jnp.logical_and(halo, i // 32 == group)
        i = jnp.where(here, jnp.where(place < 8, place - 8, place + 104), 1000)
    apart = i - j
    near, far = (8.0, 1.0) if kind == 0 else (1.0, 0.0)
    out = jnp.where(apart == 1, near, jnp.where(apart == -1, -near, 0.0))
    return out + jnp.where(apart == 2, -far, jnp.where(apart == -2, far, 0.0))


def split(x):
    high = x.astype(BF16)
    return jnp.concatenate([high, (x - high.astype(F32)).astype(BF16)], axis=1)


def suffix_tile(x):
    lane, sub = lanes(), sublanes()
    for k in (1, 2, 4):
        x = x + jnp.where(sub < 8 - k, sroll(x, -k), 0.0)
    group = jnp.broadcast_to(x[0:1, :], (8, 128))
    out, total = x, group
    for j in (1, 2, 3):
        moved = lroll(group, -32 * j)
        out = out + jnp.where(lane < 128 - 32 * j, moved, 0.0)
        total = total + moved
    return out, total


def prefix_tile(x):
    lane, sub = lanes(), sublanes()
    for k in (1, 2, 4):
        x = x + jnp.where(sub >= k, sroll(x, k), 0.0)
    group = jnp.broadcast_to(x[7:8, :], (8, 128))
    out, total = x, group
    for j in (1, 2, 3):
        moved = lroll(group, 32 * j)
        out = out + jnp.where(lane >= 32 * j, moved, 0.0)
        total = total + moved
    return out, total


def by_rows(low, high, block, fn):
    def body(n, c):
        stores = []
        for r in range(block):
            stores += fn(low + block * n + r)
        for ref, index, value in stores:
            ref[index] = value
        return c

    lax.fori_loop(0, (high - low) // block, body, 0)


def reduce_lanes(make):
    lane = lanes()

    def tree(level, start):
        if level < 0:
            return make(start)
        step = 1 << level
        a = tree(level - 1, start)
        b = tree(level - 1, start + step)
        even = (lane & step) == 0
        return jnp.where(even, a, b) + lroll(jnp.where(even, b, a), -step)

    return tree(6, 0)


def kernel(
    adj_u, adj_v, adj_t, zonal, merid, cor, thick, weight_t, target_t, atl, bottom,
    out_u, out_v, out_t,
    raw, tr, uu, vv, mask, strips_own, strips_send, strips_l, strips_r, s_raw, s_mask, s_tr,
    zx, corr, xu, xv, xb, s_xu, s_xv, s_xb, main_mat, strip_mat,
    flat, coef, flat_own, flat_l, flat_r, flat_s, ints, wt, cor_s, thick_s,
    a_src, a_dst, b_src, b_dst, y_src, y_dst, o_src, o_send, l_dst, r_dst,
    load_sem, small_sem, a_ss, a_rs, b_ss, b_rs, h_ss, h_rs, m_ss, m_rs,
):
    lon, lat, dep = lax.axis_index("lon"), lax.axis_index("lat"), lax.axis_index("dep")
    ring_y, ring_z = lon % RING_Y, lon // RING_Y

    sources = (adj_t, merid, adj_v, adj_u, zonal)
    for i in (V, T, VV, UU, U):
        def load(z, c, i=i):
            pltpu.make_async_copy(
                sources[i].at[z], raw.at[i, pl.ds(HALO, OWN), z], load_sem.at[i]
            ).start()
            return c
        if i == V:
            smalls = [
                pltpu.make_async_copy(bottom, ints.at[0], small_sem.at[0]),
                pltpu.make_async_copy(atl, ints.at[1], small_sem.at[1]),
                pltpu.make_async_copy(weight_t, wt.at[0], small_sem.at[2]),
                pltpu.make_async_copy(target_t, wt.at[1], small_sem.at[3]),
                pltpu.make_async_copy(cor, cor_s, small_sem.at[4]),
                pltpu.make_async_copy(thick, thick_s, small_sem.at[5]),
            ]
            for copy in smalls:
                copy.start()
        lax.fori_loop(0, OWN, load, 0)

    def wait_load(i):
        pltpu.make_async_copy(
            sources[i], raw.at[i, pl.ds(HALO, OWN)], load_sem.at[i]
        ).wait()

    def wrap(i, n):
        return lax.rem(i + n, n)

    def ring_y_peer(k):
        return ring_z * RING_Y + lax.rem(ring_y + k, RING_Y)

    right, left = wrap(lon + 1, NLON), wrap(lon - 1, NLON)
    above, below = wrap(lat - 1, NLAT), wrap(lat + 1, NLAT)
    first_stage = []
    for slab, to_lat in ((0, lat), (1, below), (2, above)):
        for k in range(RING_Y):
            for d in range(NDEP):
                if slab == 0 and k == 0 and d == 0:
                    continue
                to_dep = dep if d == 0 else 1 - dep
                first_stage.append((slab, 2 * k + d, d, (ring_y_peer(k), to_lat, to_dep)))
    second_stage = [
        (k, (lax.rem(lon + RING_Y * k, NLON), lat, dep)) for k in range(1, RING_Z)
    ]
    around = [
        (right, lat, dep), (left, lat, dep),
        (right, above, dep), (left, above, dep), (right, below, dep), (left, below, dep),
    ]
    barrier = pltpu.get_barrier_semaphore()
    greeted = [p[3] for p in first_stage] + [p[1] for p in second_stage] + around
    for peer in greeted:
        pl.semaphore_signal(barrier, inc=1, device_id=peer, device_id_type=MESH)

    lane, sub = lanes(), sublanes()
    for copy in smalls:
        copy.wait()
    for y in range(0, OWN, 8):
        flat[0, pl.ds(HALO + y, 8)] = ints[0, pl.ds(y, 8)].astype(F32)
        flat[1, pl.ds(HALO + y, 8)] = ints[1, pl.ds(y, 8)].astype(F32)
        turning = jnp.zeros((8, 128), F32)
        for r in range(8):
            turning = jnp.where(sub == r, cor_s[y + r], turning)
        flat[2, pl.ds(HALO + y, 8)] = turning
    thickness = jnp.zeros((8, 128), F32)
    for z in range(OWN):
        here = jnp.logical_and(sub == z % 8, lane // 32 == z // 8)
        thickness = jnp.where(here, thick_s[z], thickness)

    for kind in range(2):
        for n in range(5):
            mat = slope_matrix(kind, None if n == 0 else n - 1).astype(BF16)
            for half in range(2):
                strip_mat[kind, pl.ds(128 * half, 128), pl.ds(128 * n, 128)] = mat
                if n == 0:
                    main_mat[kind, pl.ds(128 * half, 128), :] = mat

    depth_main = [(dep * OWN + 8 * g + sub).astype(F32) for g in range(4)]
    depth_strip = (dep * OWN + 8 * (lane // 32) + sub).astype(F32)

    def row(ref, i, y):
        return jnp.broadcast_to(ref[i, pl.ds(y, 1), :], (8, 128))

    wait_load(V)

    def basin_flow(i):
        g, y = i // OWN, HALO + i % OWN
        inside = depth_main[g] < row(flat, 0, y)
        return jnp.where(inside, raw[V, y, pl.ds(8 * g, 8), :], 0.0) * row(flat, 1, y)

    level_sum = reduce_lanes(basin_flow) * thickness

    def packed(i):
        filled = jnp.concatenate([wt[i], jnp.zeros((32, 64), F32)], axis=1)
        filled = jnp.concatenate([filled, jnp.zeros((96, 128), F32)], axis=0)
        turned = filled.T
        halves = []
        for half in range(2):
            tile = turned[32 * half:32 * half + 8]
            for g in range(1, 4):
                start = 32 * half + 8 * g
                tile = jnp.where(lane // 32 == g, lroll(turned[start:start + 8], 32 * g), tile)
            halves.append(tile)
        lower = dep == 1
        return jnp.where(lower, halves[1], halves[0]), jnp.where(lower, halves[0], halves[1])

    w_own, w_other = packed(0)
    g_own, g_other = packed(1)
    deeper, whole = suffix_tile(level_sum)
    is_low = jnp.where(dep == 1, 1.0, 0.0)
    mis_own = w_own * (deeper * (1.0 / 512.0) - g_own * (1.0 / 64.0))
    mis_other = w_other * (whole * is_low * (1.0 / 512.0) - g_other * (1.0 / 64.0))
    up_own, tot_own = prefix_tile(mis_own)
    up_other, tot_other = prefix_tile(mis_other)
    a_src[0] = up_own + is_low * tot_other
    a_src[1] = up_other + (1.0 - is_low) * tot_own

    def clear(rows, tiles, few, side, slab):
        raw[:, rows] = jnp.zeros((5, HALO, 32, 128), F32)
        flat[:, rows] = jnp.zeros((3, HALO, 128), F32)
        a_dst[slab] = jnp.zeros((8, 8, 128), F32)
        y_dst[side] = jnp.zeros((HALO, 32, 128), F32)
        for ref in (strips_l, strips_r):
            ref[tiles] = jnp.zeros((10, 8, 128), F32)
        for ref in (flat_l, flat_r):
            ref[:, rows] = jnp.zeros((2, HALO, 128), F32)
        for ref in (l_dst, r_dst):
            ref[few] = jnp.zeros((2, 8, 128), F32)

    @pl.when(lat == 0)
    def _():
        clear(pl.ds(0, HALO), pl.ds(0, 10), pl.ds(0, 2), 0, 1)

    @pl.when(lat == NLAT - 1)
    def _():
        clear(pl.ds(HALO + OWN, HALO), pl.ds(50, 10), pl.ds(10, 2), 1, 2)

    pl.semaphore_wait(barrier, len(greeted))

    inner = {-1: lat > 0, 1: lat < NLAT - 1}

    def when(condition, act):
        if condition is None:
            act()
        else:
            pl.when(condition)(act)

    def send(src, dst, ss, rs, peer, toward=0):
        copy = pltpu.make_async_remote_copy(
            src_ref=src, dst_ref=dst, send_sem=ss, recv_sem=rs,
            device_id=peer, device_id_type=MESH,
        )
        when(inner.get(toward), copy.start)
        return copy, toward

    def finish(copies):
        for copy, toward in copies:
            when(inner.get(-toward), copy.wait_recv)
        for copy, toward in copies:
            when(inner.get(toward), copy.wait_send)

    a_copies = [
        send(a_src.at[d], a_dst.at[slab, slot], a_ss.at[8 * slab + slot], a_rs.at[8 * slab + slot], peer, (0, 1, -1)[slab])
        for slab, slot, d, peer in first_stage
    ]

    h_copies = []

    def halo_send(src, dst, peer, toward=0):
        n = len(h_copies)
        h_copies.append(send(src, dst, h_ss.at[n], h_rs.at[n], peer, toward))

    low, high = pl.ds(HALO, HALO), pl.ds(OWN, HALO)
    top, end = pl.ds(0, HALO), pl.ds(HALO + OWN, HALO)
    halo_send(flat.at[:, low], flat.at[:, end], (lon, above, dep), -1)
    halo_send(flat.at[:, high], flat.at[:, top], (lon, below, dep), 1)
    for i in range(2):
        for y in range(0, OWN, 8):
            tile = flat[i, pl.ds(HALO + y, 8), :]
            flat_own[i, pl.ds(y, 8), :] = pack([tile] * 4)

    def flat_sends():
        body, first, last = pl.ds(HALO, OWN), pl.ds(0, HALO), pl.ds(OWN - HALO, HALO)
        for dst, to in ((flat_l, right), (flat_r, left)):
            halo_send(flat_own, dst.at[:, body], (to, lat, dep))
            halo_send(flat_own.at[:, first], dst.at[:, end], (to, above, dep), -1)
            halo_send(flat_own.at[:, last], dst.at[:, top], (to, below, dep), 1)

    flat_sends()
    early_copies = list(h_copies)
    for first, more, n in ((T, 2, 8), (VV, 2, 7), (U, 1, 6)):
        pair = pl.ds(first, more)
        for i in range(first, first + more):
            if i != V:
                wait_load(i)
        halo_send(
            raw.at[pair, pl.ds(HALO, n)], raw.at[pair, pl.ds(HALO + OWN, n)], (lon, above, dep),
            -1,
        )
        halo_send(
            raw.at[pair, pl.ds(HALO + OWN - n, n)], raw.at[pair, pl.ds(HALO - n, n)],
            (lon, below, dep), 1,
        )

    def pack_block(n):
        stores = []
        own = {}
        for r in range(4):
            for i in range(5):
                y = HALO + 4 * n + r
                own[i, r] = pack([raw[i, y, pl.ds(8 * g, 8), :] for g in range(4)])
                stores.append((strips_own, (i, 4 * n + r), own[i, r]))
        for r in range(5):
            tiles = [own[i, r] for i in range(4)] if r < 4 else [own[U, q] for q in range(4)]
            to_right, to_left = pack_four(tiles)
            stores.append((strips_send, (0, 5 * n + r), to_right))
            stores.append((strips_send, (1, 5 * n + r), to_left))
        return stores

    by_rows(0, OWN // 4, 1, pack_block)

    def strip_sends(put, src_r, src_l, dst_l, dst_r, edge):
        body = src_r.shape[-3] if len(src_r.shape) == 3 else src_r.shape[-2]
        sl = (slice(None),) * (0 if len(src_r.shape) == 3 else 1)
        here, first, last = pl.ds(edge, body), pl.ds(0, edge), pl.ds(body - edge, edge)
        after = pl.ds(body + edge, edge)
        put(src_r, dst_l.at[sl + (here,)], (right, lat, dep))
        put(src_l, dst_r.at[sl + (here,)], (left, lat, dep))
        put(src_r.at[sl + (first,)], dst_l.at[sl + (after,)], (right, above, dep), -1)
        put(src_l.at[sl + (first,)], dst_r.at[sl + (after,)], (left, above, dep), -1)
        put(src_r.at[sl + (last,)], dst_l.at[sl + (first,)], (right, below, dep), 1)
        put(src_l.at[sl + (last,)], dst_r.at[sl + (first,)], (left, below, dep), 1)

    strips_from = len(h_copies)
    strip_sends(halo_send, strips_send.at[0], strips_send.at[1], strips_l, strips_r, 10)
    early_copies += h_copies[strips_from:strips_from + 2]
    late_copies = h_copies[len(early_copies) - 2:strips_from] + h_copies[strips_from + 2:]

    finish(a_copies)
    a_dst[0, 0] = a_src[0]
    sums = []
    for slab in range(3):
        total = a_dst[slab, 0]
        for k in range(1, 8):
            total = total + a_dst[slab, k]
        sums.append(total)
    b_src[0] = sums[0]
    b_src[1] = jnp.where(lane % 32 >= 16, sums[1], sums[2])
    b_copies = [
        send(b_src, b_dst.at[k], b_ss.at[k], b_rs.at[k], peer) for k, peer in second_stage
    ]

    def prepare_row(y):
        deep = row(flat, 0, y)
        stores = []
        for g in range(4):
            at = pl.ds(8 * g, 8)
            inside = depth_main[g] < deep
            stores += [
                (mask, (y, at), jnp.where(inside, 1.0 / 12.0, 0.0)),
                (tr, (0, y, at), jnp.where(inside, raw[T, y, at, :], 0.0)),
                (uu, (y, at), jnp.where(inside, 3.0 * raw[UU, y, at, :], 0.0)),
            ]
        return stores

    by_rows(HALO, HALO + OWN, 4, prepare_row)

    finish(early_copies)
    has_above = jnp.where(lat > 0, 1.0, 0.0)
    has_below = jnp.where(lat < NLAT - 1, 1.0, 0.0)
    flat[0, top] = flat[0, top] * has_above
    flat[0, end] = flat[0, end] * has_below
    for y in range(0, ROWS, 8):
        at = pl.ds(y, 8)
        turning = flat[2, at]
        real, imag = jnp.ones((8, 128), F32), jnp.zeros((8, 128), F32)
        for k in range(9):
            coef[2 * k, at] = real
            coef[2 * k + 1, at] = imag
            real, imag = real - turning * imag, imag + turning * real
    for i in range(2):
        for y in range(0, ROWS, 8):
            at = pl.ds(y, 8)
            own = pack([flat[i, at, :]] * 4)
            flat_s[i, at, :] = merge(own, flat_l[i, at, :], flat_r[i, at, :])
    flat_s[0, top] = flat_s[0, top] * has_above
    flat_s[0, end] = flat_s[0, end] * has_below

    def strip_block(n, own):
        stores = []
        for r in range(4):
            y = 4 * n + r
            inside = depth_strip < row(flat_s, 0, y)
            stores.append((s_mask, y, jnp.where(inside, 1.0 / 12.0, 0.0)))
            for i in range(5):
                at, slot = (5 * n + r, i) if i < 4 else (5 * n + 4, r)
                tile = merge(own(i, r), strips_l[at], strips_r[at], slot, slot)
                if i == T:
                    stores.append((s_tr, (0, y), jnp.where(inside, tile, 0.0)))
                    continue
                if i == UU:
                    tile = jnp.where(inside, 3.0 * tile, 0.0)
                stores.append((s_raw, (i, y), tile))
        return stores

    by_rows(
        2, 10, 1, lambda n: strip_block(n, lambda i, r: strips_own[i, 4 * n + r - HALO])
    )
    def slope(kind, ranges, main, strip, main_out, strip_out, fold):
        at = [pl.ds(low, high - low) for low, high in ranges]
        sizes = [high - low for low, high in ranges]
        got = jnp.dot(
            jnp.concatenate([split(strip(a).reshape(8 * n, 128)) for a, n in zip(at, sizes)], axis=0),
            strip_mat[kind], preferred_element_type=F32,
        )
        edges = []
        start = 0
        for a, n in zip(at, sizes):
            mine = got[8 * start:8 * (start + n)]
            start += n
            strip_out[a] = mine[:, :128].reshape(n, 8, 128)
            edges.append([
                mine[:, 128 * g + 128:128 * g + 256].reshape(n, 8, 128) for g in range(4)
            ])
            if not fold:
                for g in range(4):
                    corr[g, a] = edges[-1][g]

        def emit(a, out, mine):
            if fold:
                out = out + jnp.concatenate(mine, axis=1)
            main_out[a] = out

        if len(ranges) > 1:
            out = jnp.dot(
                jnp.concatenate(
                    [split(main(a).reshape(32 * n, 128)) for a, n in zip(at, sizes)], axis=0
                ),
                main_mat[kind], preferred_element_type=F32,
            )
            start = 0
            for a, n, mine in zip(at, sizes, edges):
                emit(a, out[32 * start:32 * (start + n)].reshape(n, 32, 128), mine)
                start += n
            return
        part = sizes[0] // 4
        for n in range(4):
            a = pl.ds(ranges[0][0] + part * n, part)
            out = jnp.dot(
                split(main(a).reshape(32 * part, 128)), main_mat[kind],
                preferred_element_type=F32,
            ).reshape(part, 32, 128)
            emit(a, out, [e[part * n:part * n + part] for e in edges[0]])

    def fixed_slopes(*ranges):
        slope(1, ranges, lambda at: uu[at], lambda at: s_raw[UU, at], xu, s_xu, True)
        slope(
            1, ranges, lambda at: 36.0 * mask[at] * raw[VV, at],
            lambda at: 36.0 * s_mask[at] * s_raw[VV, at], xv, s_xv, True,
        )
        slope(
            1, ranges, lambda at: mask[at] * flat[1, at][:, None, :],
            lambda at: s_mask[at] * flat_s[1, at][:, None, :], xb, s_xb, True,
        )

    fixed_slopes((HALO, HALO + OWN))

    finish(b_copies)
    ups = []
    for i in range(2):
        total = b_src[i]
        for k in range(1, RING_Z):
            total = total + b_dst[k, i]
        ups.append(total * thickness * 4.5)

    def gradient(y, up, offset):
        moved = pltpu.roll(up, lax.rem(256 + offset - y, 128), 1)
        spreads = [jnp.broadcast_to(moved[:, 32 * g:32 * g + 1], (8, 128)) for g in range(4)]
        basin = row(flat, 1, y)
        stores = []
        for g in range(4):
            at = pl.ds(8 * g, 8)
            value = mask[y, at, :] * (36.0 * raw[VV, y, at, :] + basin * spreads[g])
            stores.append((vv, (y, at), value))
            stores.append((xv, (y, at), xv[y, at, :] + spreads[g] * xb[y, at, :]))
        joined = spreads[0]
        for g in range(1, 4):
            joined = jnp.where(lane // 32 == g, spreads[g], joined)
        value = s_mask[y] * (36.0 * s_raw[VV, y] + row(flat_s, 1, y) * joined)
        stores.append((s_raw, (VV, y), value))
        stores.append((s_xv, y, s_xv[y] + joined * s_xb[y]))
        return stores

    by_rows(HALO, HALO + OWN, 4, lambda y: gradient(y, ups[0], HALO))
    def column(k, low, high, last, get, emit):
        flux, held, vs, power = {}, {}, {}, {}

        def reach(y):
            held[y] = get("t", y)
            flux[y] = get("V", y) * held[y]

        def turn(y):
            if k == 0:
                vs[y] = get("v", y)
            else:
                power[y] = row(coef, 2 * k, y), row(coef, 2 * k + 1, y)
                vs[y] = power[y][0] * get("v", y) + power[y][1] * get("u", y)

        for y in range(low - 2, low + 2):
            reach(y)
        for y in (low - 1, low):
            turn(y)
        for y in range(low, high):
            reach(y + 2)
            turn(y + 1)
            z_x = get("zx", y)
            if k == 0:
                z_x = z_x + get("xu", y)
            else:
                z_x = z_x + (power[y][0] * get("xu", y) - power[y][1] * get("xv", y))
            z_y = 8.0 * (flux[y + 1] - flux[y - 1]) + (vs[y + 1] - vs[y - 1])
            z_y = z_y - (flux[y + 2] - flux[y - 2])
            scale = (1.0 / 12.0) if last else get("m", y)
            emit(y, held[y] + scale * (z_x + z_y))

    def step(k, ranges, last):
        now, new = k % 2, 1 - k % 2
        slope(
            0, ranges, lambda at: raw[U, at] * tr[now, at],
            lambda at: s_raw[U, at] * s_tr[now, at], zx, corr.at[4], False,
        )

        def strip_get(what, y):
            return {
                "t": lambda: s_tr[now, y], "u": lambda: s_raw[UU, y], "v": lambda: s_raw[VV, y],
                "m": lambda: s_mask[y], "V": lambda: s_raw[V, y],
                "zx": lambda: corr[4, y], "xu": lambda: s_xu[y], "xv": lambda: s_xv[y],
            }[what]()

        def strip_emit(y, value):
            s_tr[new, y] = value

        if not last:
            for low, high in ranges:
                column(k, low, high, False, strip_get, strip_emit)

        def group(g, c):
            at = pl.ds(pl.multiple_of(8 * g, 8), 8)

            def get(what, y):
                return {
                    "t": lambda: tr[now, y, at, :], "u": lambda: uu[y, at, :],
                    "v": lambda: vv[y, at, :], "m": lambda: mask[y, at, :],
                    "V": lambda: raw[V, y, at, :],
                    "zx": lambda: zx[y, at, :] + corr[g, y],
                    "xu": lambda: xu[y, at, :], "xv": lambda: xv[y, at, :],
                }[what]()

            def emit(y, value):
                if last:
                    out_t[y - HALO, at, :] = value
                else:
                    tr[new, y, at, :] = value

            for low, high in ranges:
                column(k, low, high, last, get, emit)
            return c

        lax.fori_loop(0, 4, group, 0, unroll=4)

    def inner_rows(k, last):
        for n in range(1, 5):
            step(k + n - 1, ((HALO + 2 * n, HALO + OWN - 2 * n),), last and n == 4)

    def outer_rows(k, last):
        for n in range(1, 5):
            low, high = 2 * n, ROWS - 2 * n
            step(k + n - 1, ((low, low + HALO), (high - HALO, high)), last and n == 4)

    inner_rows(0, False)
    finish(late_copies[:6])
    by_rows(0, HALO, 4, prepare_row)
    by_rows(HALO + OWN, ROWS, 4, prepare_row)
    for outer in (0, ROWS - 2):
        raw[U, pl.ds(outer, 2)] = jnp.zeros((2, 32, 128), F32)
    for outer in (0, ROWS - 1):
        raw[pl.ds(2, 2), outer] = jnp.zeros((2, 32, 128), F32)

    def pack_outer(shift):
        return lambda n: [
            (strips_own, (i, 4 * n + r + shift),
             pack([raw[i, 4 * n + r, pl.ds(8 * g, 8), :] for g in range(4)]))
            for r in range(4) for i in range(5)
        ]

    by_rows(0, 2, 1, pack_outer(OWN))
    by_rows(10, 12, 1, pack_outer(0))
    finish(late_copies[6:])
    def strip_outer(shift):
        return lambda n: strip_block(n, lambda i, r: strips_own[i, 4 * n + r + shift])

    by_rows(0, 2, 1, strip_outer(OWN))
    by_rows(10, 12, 1, strip_outer(0))

    fixed_slopes((2, HALO), (HALO + OWN, ROWS - 2))
    by_rows(0, HALO, 4, lambda y: gradient(y, ups[1], HALO - OWN))
    by_rows(HALO + OWN, ROWS, 4, lambda y: gradient(y, ups[1], HALO + OWN))
    outer_rows(0, False)

    m_copies = []

    def mid_send(src, dst, peer, toward=0):
        n = len(m_copies)
        m_copies.append(send(src, dst, m_ss.at[n], m_rs.at[n], peer, toward))

    y_src[0] = tr[0, low]
    y_src[1] = tr[0, high]
    mid_send(y_src.at[0], y_dst.at[1], (lon, above, dep), -1)
    mid_send(y_src.at[1], y_dst.at[0], (lon, below, dep), 1)

    def pack_tracer(n):
        own = [
            pack([tr[0, HALO + 4 * n + r, pl.ds(8 * g, 8), :] for g in range(4)])
            for r in range(4)
        ]
        both = pack_four(own)
        return [(o_src, 4 * n + r, own[r]) for r in range(4)] + [
            (o_send, (i, n), both[i]) for i in range(2)
        ]

    by_rows(0, OWN // 4, 2, pack_tracer)
    strip_sends(mid_send, o_send.at[0], o_send.at[1], l_dst, r_dst, 2)

    def turned(y):
        stores = []
        real, imag = row(coef, 16, y) * (1.0 / 3.0), row(coef, 17, y) * (1.0 / 3.0)
        for g in range(4):
            at = pl.ds(8 * g, 8)
            u_0, v_0 = uu[y, at, :], vv[y, at, :]
            stores.append((out_u, (y - HALO, at), real * u_0 - imag * v_0))
            stores.append((out_v, (y - HALO, at), real * v_0 + imag * u_0))
        return stores

    by_rows(HALO, HALO + OWN, 4, turned)

    finish(m_copies[2:4])

    def own_block(n):
        return [
            (s_tr, (0, HALO + 4 * n + r), merge(o_src[4 * n + r], l_dst[2 + n], r_dst[2 + n], r, r))
            for r in range(4)
        ]

    by_rows(0, OWN // 4, 2, own_block)
    inner_rows(4, True)
    finish(m_copies[:2] + m_copies[4:])

    def halo_block(n):
        stores = []
        for r in range(4):
            for side, at, block, valid in (
                (0, 4 * n + r, n, has_above),
                (1, HALO + OWN + 4 * n + r, 10 + n, has_below),
            ):
                tiles = [y_dst[side, 4 * n + r, pl.ds(8 * g, 8), :] * valid for g in range(4)]
                stores += [(tr, (0, at, pl.ds(8 * g, 8)), tiles[g]) for g in range(4)]
                strip = merge(pack(tiles), l_dst[block] * valid, r_dst[block] * valid, r, r)
                stores.append((s_tr, (0, at), strip))
        return stores

    by_rows(0, 2, 1, halo_block)
    outer_rows(4, True)


def store(*refs):
    held, outs, sem = refs[:3], refs[3:6], refs[6]
    for n in range(3):
        def level(z, c, n=n):
            pltpu.make_async_copy(held[n].at[:, z], outs[n].at[z], sem.at[n]).start()
            return c
        lax.fori_loop(0, OWN, level, 0)
    for n in range(3):
        pltpu.make_async_copy(held[n], outs[n], sem.at[n]).wait()


def per_device(*args):
    args = args[:7] + (args[7].T, args[8].T) + args[9:]
    held = pltpu.VMEM((32, 32, 128), F32)
    main = pltpu.VMEM((ROWS, 32, 128), F32)
    strip = pltpu.VMEM((ROWS, 8, 128), F32)
    dma = pltpu.SemaphoreType.DMA
    results = pl.pallas_call(
        kernel,
        out_shape=(held,) * 3,
        in_specs=[pl.BlockSpec(memory_space=pltpu.HBM)] * 11,
        out_specs=(pl.BlockSpec(memory_space=pltpu.VMEM),) * 3,
        scratch_shapes=[
            pltpu.VMEM((5, ROWS, 32, 128), F32),
            pltpu.VMEM((2, ROWS, 32, 128), F32),
            main, main, main,
            pltpu.VMEM((5, ROWS, 8, 128), F32),
            pltpu.VMEM((2, 40, 8, 128), F32),
            pltpu.VMEM((60, 8, 128), F32),
            pltpu.VMEM((60, 8, 128), F32),
            pltpu.VMEM((5, ROWS, 8, 128), F32),
            strip,
            pltpu.VMEM((2, ROWS, 8, 128), F32),
            main,
            pltpu.VMEM((5, ROWS, 8, 128), F32),
            main, main, main, strip, strip, strip,
            pltpu.VMEM((2, 256, 128), BF16),
            pltpu.VMEM((2, 256, 640), BF16),
            pltpu.VMEM((3, ROWS, 128), F32),
            pltpu.VMEM((18, ROWS, 128), F32),
            pltpu.VMEM((2, OWN, 128), F32),
            pltpu.VMEM((2, ROWS, 128), F32),
            pltpu.VMEM((2, ROWS, 128), F32),
            pltpu.VMEM((2, ROWS, 128), F32),
            pltpu.VMEM((2, OWN, 128), jnp.int32),
            pltpu.VMEM((2, 32, 64), F32),
            pltpu.SMEM((32,), F32),
            pltpu.SMEM((32,), F32),
            pltpu.VMEM((2, 8, 128), F32),
            pltpu.VMEM((3, 8, 8, 128), F32),
            pltpu.VMEM((2, 8, 128), F32),
            pltpu.VMEM((8, 2, 8, 128), F32),
            pltpu.VMEM((2, HALO, 32, 128), F32),
            pltpu.VMEM((2, HALO, 32, 128), F32),
            pltpu.VMEM((OWN, 8, 128), F32),
            pltpu.VMEM((2, 8, 8, 128), F32),
            pltpu.VMEM((12, 8, 128), F32),
            pltpu.VMEM((12, 8, 128), F32),
            dma((5,)), dma((6,)), dma((24,)), dma((24,)), dma((8,)), dma((8,)),
            dma((20,)), dma((20,)), dma((8,)), dma((8,)),
        ],
        compiler_params=pltpu.CompilerParams(
            collective_id=0, has_side_effects=True, vmem_limit_bytes=60 * 1024 * 1024
        ),
        name="adjoint",
    )(*args)
    return pl.pallas_call(
        store,
        out_shape=(jax.ShapeDtypeStruct((32, 32, 128), F32),) * 3,
        in_specs=[pl.BlockSpec(memory_space=pltpu.VMEM)] * 3,
        out_specs=(pl.BlockSpec(memory_space=pltpu.HBM),) * 3,
        scratch_shapes=[dma((3,))],
        compiler_params=pltpu.CompilerParams(vmem_limit_bytes=4 * 1024 * 1024),
        name="store",
    )(*results)


def solution(mesh):
    block, level = P("dep", "lat", "lon"), P(None, "lat")
    in_specs = (block,) * 5 + (P("lat"), P("dep"), level, level) + (P("lat", "lon"),) * 2
    return jax.shard_map(
        per_device, mesh=mesh, in_specs=in_specs, out_specs=(block,) * 3, check_vma=False
    )
```
